32 devices in a mesh: beam: 2 (over y), height: 4 (over x, core), angles: 4 (over z).
Axes of the slice: x: 2, y: 2, z: 4, core: 2. Of those that a mesh axis runs over, the one named last changes fastest.
Arguments:
- element_maps: float32 [24, 4, 32, 256], P(None, 'height', 'beam'), may hold values from 0.1 to 1
- angles: int32 [8], P('angles'), may hold values from 0 to 95
- absorb_incident: float32 [24], replicated, may hold values from 0.0003 to 0.003
- absorb_table: float32 [32, 24], replicated, may hold values from 0.0003 to 0.003
- line_index: int32 [24], replicated, may hold values from 0 to 31
- measured: float32 [8, 24, 4, 256], P('angles', None, 'height'), may hold values from 0 to 1
Outputs:
- updated_maps: float32 [24, 4, 32, 256], P(None, 'height', 'beam')
- residual: float32 [8, 24, 4, 256], P('angles', None, 'height')
The draws below stay inside these ranges and needn't reach their ends.
All inputs are finite; a program needn't handle non-finite values.
Results may differ from the reference program's by a relative error of at most 0.0003.
Values sent between devices are 32-bit elements; how exact they have to be, the bound alone decides.
A program may use at most 64 MiB of HBM per device.

```python
import math
import jax
import jax.numpy as jnp
from jax import lax

E = 24
LINES = 32
NY = 256
WINDOW = 96
ITERS = 2
NX = 32
NZ = 4
A_TOTAL = 8


def set_ends(array, stream_key, least, top_value):
    place = [jax.random.randint(jax.random.fold_in(stream_key, axis), (), 0, length) for axis, length in enumerate(array.shape)]
    longest = array.shape.index(max(array.shape))
    beside = place[:longest] + [(place[longest] + 1) % array.shape[longest]] + place[longest + 1:]
    return array.at[tuple(place)].set(least).at[tuple(beside)].set(top_value)


def level_of(own_key, dims, cuts, smallest, high):
    gain = 1.0
    for axis_at, blocks in cuts:
        draws = jax.random.uniform(jax.random.fold_in(jax.random.fold_in(own_key, 6), axis_at), (blocks,), jnp.float32, smallest / len(cuts), high / len(cuts))
        gain = gain * jnp.repeat(jnp.exp(draws), dims[axis_at] // blocks).reshape((-1,) + (1,) * (len(dims) - 1 - axis_at))
    return gain


def setup_inputs(seed: int = 0) -> dict:
    arg_keys = jax.random.split(jax.random.key(seed), 7)
    return {
        "element_maps": jnp.clip(jnp.exp(math.log(1.0) - 2.3025851 * jax.random.uniform(arg_keys[0], (E, NZ, NX, NY), jnp.float32) ** level_of(arg_keys[0], (E, NZ, NX, NY), ((1, 4), (2, 2)), -0.2, 0.2)), 0.1, 1.0),
        "angles": set_ends(jax.random.randint(arg_keys[1], (A_TOTAL,), 0, WINDOW), jax.random.fold_in(arg_keys[1], 1), 0, WINDOW - 1).astype(jnp.int32),
        "absorb_incident": jnp.clip(jnp.exp(jax.random.uniform(arg_keys[2], (E,), jnp.float32, math.log(0.0003), math.log(0.003))), 0.0003, 0.003),
        "absorb_table": jnp.clip(jnp.exp(jax.random.uniform(arg_keys[3], (LINES, E), jnp.float32, math.log(0.0003), math.log(0.003))), 0.0003, 0.003),
        "line_index": set_ends(jax.random.randint(arg_keys[4], (E,), 0, LINES), jax.random.fold_in(arg_keys[4], 1), 0, LINES - 1).astype(jnp.int32),
        "measured": jnp.clip(1.0 * jax.random.uniform(arg_keys[5], (A_TOTAL, E, NZ, NY), jnp.float32) ** level_of(arg_keys[5], (A_TOTAL, E, NZ, NY), ((0, 4), (2, 4)), -0.2, 0.2), 0.0, 1.0),
    }


EPSILON = 1e-06
STEP_SIZE = 0.05
DETECT_SCALE = 1.0 / 32.0

def sample(grid, x_pos, slope_one):
    row_width = grid.shape[3]
    position = jnp.arange(row_width).astype(grid.dtype)[None, :] + x_pos[:, None] * slope_one
    floor_pos = jnp.floor(position)
    fraction = position - floor_pos
    left_index = floor_pos.astype(jnp.int32)

    def take_side(offset):
        column = left_index + offset
        inside = (column >= 0) & (column < row_width)
        clipped = jnp.clip(column, 0, row_width - 1)
        values = jnp.take_along_axis(grid, jnp.broadcast_to(clipped, grid.shape), axis=3)
        return jnp.where(inside, values, jnp.zeros_like(values))
    return take_side(0) * (1.0 - fraction) + take_side(1) * fraction

def signal(grid, angle_one, absorb_incident, absorb_out):
    angle_rad = ((angle_one.astype(grid.dtype) + 0.5) / WINDOW - 0.5) * (math.pi / 2)
    slope_one = jnp.tan(angle_rad)
    path_one = 1.0 / jnp.cos(angle_rad)
    beam_len = grid.shape[2]
    x_pos = jnp.arange(beam_len).astype(grid.dtype) - (beam_len - 1) / 2
    sampled = sample(grid, x_pos, slope_one)
    mu_in = path_one * jnp.einsum('e,ezxy->zxy', absorb_incident, sampled, precision=lax.Precision.HIGHEST)
    tau_in = jnp.cumsum(mu_in, axis=1) - 0.5 * mu_in
    mu_out = jnp.einsum('ej,jzxy->ezxy', absorb_out, sampled, precision=lax.Precision.HIGHEST)
    tau_out = jnp.flip(jnp.cumsum(jnp.flip(mu_out, 3), axis=3), 3) - 0.5 * mu_out
    return path_one * DETECT_SCALE * lax.optimization_barrier(jnp.sum(sampled * jnp.exp(-tau_in[None] - tau_out), axis=2))

def reference(element_maps, angles, absorb_incident, absorb_table, line_index, measured):
    absorb_out = absorb_table[line_index]
    current = element_maps
    residual = jnp.zeros_like(measured)
    for iteration in range(ITERS):

        def one_angle(gradient, item):
            angle_one, seen_one = item
            fluor, pull_back = jax.vjp(lambda grid: signal(grid, angle_one, absorb_incident, absorb_out), current)
            misfit = fluor - seen_one
            return (gradient + pull_back(misfit)[0], misfit)
        gradient, residual = lax.scan(one_angle, jnp.zeros_like(current), (angles, measured))
        scale_norm = jnp.sqrt(jnp.mean(gradient * gradient) + EPSILON)
        current = current - STEP_SIZE * gradient / scale_norm
    return (current, residual)
```

```python
import functools
import math

import jax
import jax.numpy as jnp
from jax import lax
from jax.experimental import pallas as pl
from jax.experimental.pallas import tpu as pltpu
from jax.sharding import PartitionSpec as P

WINDOW = 96
ITERS = 2
EPSILON = 1e-06
STEP_SIZE = 0.05
DETECT_SCALE = 1.0 / 32.0
HIGHEST = lax.Precision.HIGHEST
MESH = pl.DeviceIdType.MESH
F32 = jnp.float32
BF16 = jnp.bfloat16
GROUP = 8


def split(value):
    high = value.astype(BF16)
    return high, (value - high.astype(F32)).astype(BF16)


def dot(left, right):
    return jnp.dot(left, right, preferred_element_type=F32)


def mix(high_ref, low_ref, value):
    high, low = split(value)
    return dot(high_ref[...], high) + (dot(low_ref[...], high) + dot(high_ref[...], low))


def spread(value, sums):
    high, low = split(value)
    return dot(high, sums) + dot(low, sums)


def kernel(
    sizes,
    maps_ref, info_ref, measured_ref, incident_ref,
    out_high, out_low, back_high, back_low, exit_ref, enter_ref,
    current, residual_ref,
    shifted, info, seen, scalars, coef0, coef1, sampled, fading, slabs, misfit,
    acc0, acc1, squares,
    local_sem, info_send, info_recv, seen_send, seen_recv,
    slab_send, slab_recv, norm_send, norm_recv,
):
    beams, heights, groups = sizes
    elems, width = maps_ref.shape[1:]
    depth = maps_ref.shape[0]
    mine = info_ref.shape[0]
    total_angles = groups * mine
    xgroups = depth // GROUP
    rows = GROUP * elems
    beam = lax.axis_index("beam")
    height = lax.axis_index("height")
    group = lax.axis_index("angles")
    plane = beams * heights
    place = beam * heights + height
    cells = float(elems * depth * width * plane)

    def plane_id(index):
        return (index // heights, lax.rem(index, heights), group)

    barrier = pltpu.get_barrier_semaphore()
    for step in range(1, groups):
        pl.semaphore_signal(
            barrier, inc=1, device_id=(beam, height, lax.rem(group + step, groups)), device_id_type=MESH
        )

    @pl.loop(1, plane)
    def _(step):
        pl.semaphore_signal(
            barrier, inc=1, device_id=plane_id(lax.rem(place + step, plane)), device_id_type=MESH
        )

    pl.semaphore_wait(barrier, groups - 1 + plane - 1)

    def info_copy(step, slot):
        peer = lax.rem(group + step, groups)
        part = pl.ds(slot * mine, mine)
        return pltpu.make_async_remote_copy(
            info_ref, info.at[part], info_send.at[peer], info_recv.at[slot],
            device_id=(beam, height, peer), device_id_type=MESH,
        )

    def seen_copy(step, slot):
        peer = lax.rem(group + step, groups)
        part = pl.ds(slot * mine, mine)
        return pltpu.make_async_remote_copy(
            measured_ref, seen.at[part], seen_send.at[peer], seen_recv.at[slot],
            device_id=(beam, height, peer), device_id_type=MESH,
        )

    for step in range(1, groups):
        info_copy(step, group).start()
    for step in range(1, groups):
        seen_copy(step, group).start()
    info[pl.ds(group * mine, mine)] = info_ref[...]
    seen[pl.ds(group * mine, mine)] = measured_ref[...]

    for x in range(depth):
        plane_x = maps_ref[x]
        current[x] = plane_x
        shifted[x] = pltpu.roll(plane_x, width - 1, 1)

    for step in range(1, groups):
        copy = info_copy(step, lax.rem(group + step, groups))
        copy.wait_send()
        copy.wait_recv()
    fill = pltpu.make_async_copy(info, scalars, local_sem)
    fill.start()
    fill.wait()

    def slab_copy(iteration, a, step, slot):
        peer = lax.rem(beam + step, beams)
        return pltpu.make_async_remote_copy(
            slabs.at[iteration, beam, a], slabs.at[iteration, slot, a],
            slab_send.at[iteration, peer, a], slab_recv.at[iteration, slot, a],
            device_id=(peer, height, group), device_id_type=MESH,
        )

    def norm_copy(iteration, step, slot):
        peer = lax.rem(place + step, plane)
        return pltpu.make_async_remote_copy(
            squares.at[iteration, place], squares.at[iteration, slot],
            norm_send.at[iteration, peer], norm_recv.at[iteration, slot],
            device_id=plane_id(peer), device_id_type=MESH,
        )

    def forward(iteration, a):
        cols = info[a]
        start = jnp.broadcast_to(cols[:, 0:1], (depth, width))
        fraction = cols[:, 1:2]
        path = cols[0:1, 2:3]
        position = lax.broadcasted_iota(jnp.int32, (depth, width), 1).astype(F32)
        below = start < 0
        inside = (below & (position <= (width - 1) + start)) | (~below & (position >= start))
        edge = below & (position == width - 1) & (start >= -width)
        inner = inside & (position <= width - 2)
        coef0[a] = jnp.where(inside, 1.0 - fraction, 0.0)
        coef1[a] = jnp.where(inner | edge, fraction, 0.0)
        carry = jnp.zeros((1, width), F32)
        total = jnp.zeros((elems, width), F32)
        for g in range(xgroups):
            for xi in range(GROUP):
                x = g * GROUP + xi
                blend = coef0[a, x : x + 1] * current[x] + coef1[a, x : x + 1] * shifted[x]
                shift = scalars[a, x, 3].astype(jnp.int32)
                sampled[a, x * elems : (x + 1) * elems] = pltpu.roll(blend, shift, 1)
            mu = mix(out_high, out_low, sampled[a, g * rows : (g + 1) * rows])
            depth_in = path * mu[rows : rows + GROUP] + carry
            carry = carry + path * mu[rows + GROUP : rows + GROUP + 1]
            tau = spread(mu[:rows], exit_ref[...])
            for xi in range(GROUP):
                x = g * GROUP + xi
                fade = jnp.exp(-(tau[xi * elems : (xi + 1) * elems] + depth_in[xi : xi + 1]))
                fading[a, x * elems : (x + 1) * elems] = fade
                total = total + fade * sampled[a, x * elems : (x + 1) * elems]
        slabs[iteration, beam, a, 0:elems] = (path * DETECT_SCALE) * total
        slabs[iteration, beam, a, elems : elems + 8] = jnp.broadcast_to(carry, (8, width))
        for step in range(1, beams):
            slab_copy(iteration, a, step, beam).start()

    def backward(iteration, a):
        for step in range(1, beams):
            copy = slab_copy(iteration, a, step, lax.rem(beam + step, beams))
            copy.wait_send()
            copy.wait_recv()
        cols = info[a]
        path = cols[0:1, 2:3]
        before = jnp.zeros((1, width), F32)
        scale = jnp.zeros((1, width), F32)
        fluor = jnp.zeros((elems, width), F32)
        after = jnp.zeros((elems, width), F32)
        for b in range(beams):
            dim = jnp.exp(-before)
            part = dim * slabs[iteration, b, a, 0:elems]
            fluor = fluor + part
            after = after + jnp.where(b > beam, 1.0, 0.0) * part
            scale = scale + jnp.where(b == beam, 1.0, 0.0) * dim
            before = before + slabs[iteration, b, a, elems : elems + 1]
        residual = fluor - seen[a]
        misfit[a] = residual
        carry = jnp.sum(residual * after, axis=0, keepdims=True)
        source = residual * (scale * (path * DETECT_SCALE))
        incident = path * incident_ref[...]
        for g in reversed(range(xgroups)):
            emitted = []
            for xi in range(GROUP):
                x = g * GROUP + xi
                part = slice(x * elems, (x + 1) * elems)
                emitted.append(source * fading[a, part] * sampled[a, part])
            mixed = mix(back_high, back_low, jnp.concatenate(emitted, axis=0))
            behind = mixed[rows : rows + GROUP] + carry
            carry = carry + mixed[rows + GROUP : rows + GROUP + 1]
            back = spread(mixed[:rows], enter_ref[...])
            for xi in range(GROUP):
                x = g * GROUP + xi
                weighted = source * fading[a, x * elems : (x + 1) * elems]
                grad = (
                    weighted
                    - incident * behind[xi : xi + 1]
                    - back[xi * elems : (xi + 1) * elems]
                )
                shift = scalars[a, x, 4].astype(jnp.int32)
                grad = pltpu.roll(grad, shift, 1)
                acc0[x] = acc0[x] + coef0[a, x : x + 1] * grad
                acc1[x] = acc1[x] + coef1[a, x : x + 1] * grad

    @pl.loop(0, ITERS)
    def _(iteration):
        @pl.loop(0, total_angles)
        def _(a):
            forward(iteration, a)

        @pl.when(iteration == 0)
        def _():
            for step in range(1, groups):
                copy = seen_copy(step, lax.rem(group + step, groups))
                copy.wait_send()
                copy.wait_recv()

        acc0[...] = jnp.zeros_like(acc0)
        acc1[...] = jnp.zeros_like(acc1)

        @pl.loop(0, total_angles)
        def _(a):
            backward(iteration, a)

        square = jnp.zeros((8, width), F32)
        for x in range(depth):
            grad = acc0[x] + pltpu.roll(acc1[x], 1, 1)
            acc0[x] = grad
            grad = grad * grad
            for row in range(0, elems, 8):
                square = square + grad[row : row + 8]
        folded = square[:, 0:128]
        for lane in range(128, width, 128):
            folded = folded + square[:, lane : lane + 128]
        squares[iteration, place] = folded

        @pl.loop(1, plane)
        def _(step):
            norm_copy(iteration, step, place).start()

        @pl.loop(1, plane)
        def _(step):
            copy = norm_copy(iteration, step, lax.rem(place + step, plane))
            copy.wait_send()
            copy.wait_recv()

        whole = jnp.sum(squares[iteration], axis=0)
        whole = jnp.sum(jnp.sum(whole, axis=0, keepdims=True), axis=1, keepdims=True)
        rate = STEP_SIZE / jnp.sqrt(whole / cells + EPSILON)
        for x in range(depth):
            plane_x = current[x] - rate * acc0[x]
            current[x] = plane_x
            shifted[x] = pltpu.roll(plane_x, width - 1, 1)

    residual_ref[...] = misfit[pl.ds(group * mine, mine)]


def shards(element_maps, angles, absorb_incident, absorb_table, line_index, measured):
    elems, height_rows, depth, width = element_maps.shape
    beams = lax.axis_size("beam")
    heights = lax.axis_size("height")
    groups = lax.axis_size("angles")
    mine = angles.shape[0]
    total_angles = groups * mine
    line_total = depth * beams
    rows = GROUP * elems

    pick_line = (line_index[:, None] == jnp.arange(absorb_table.shape[0])[None, :]).astype(F32)
    absorb_out = jnp.dot(pick_line, absorb_table, precision=HIGHEST)
    eye = jnp.eye(GROUP, dtype=F32)
    places = jnp.arange(GROUP)
    earlier = (places[:, None] > places[None, :]).astype(F32) + 0.5 * eye
    ones = jnp.ones((8, GROUP), F32)

    def stack(table, sums, vector):
        body = (eye[:, None, :, None] * table[None, :, None, :]).reshape(rows, rows)
        tail = jnp.concatenate([sums, ones], axis=0)
        tail = (tail[:, :, None] * vector[None, None, :]).reshape(GROUP + 8, rows)
        return split(jnp.concatenate([body, tail], axis=0))

    out_high, out_low = stack(absorb_out, earlier, absorb_incident)
    back_high, back_low = stack(absorb_out.T, earlier.T, jnp.ones_like(absorb_incident))
    later = jnp.arange(width)
    exit_sum = (later[:, None] > later[None, :]).astype(F32) + 0.5 * (
        later[:, None] == later[None, :]
    ).astype(F32)

    x_pos = (lax.axis_index("beam") * depth + jnp.arange(depth)).astype(F32) - (line_total - 1) / 2
    angle_rad = ((angles.astype(F32) + 0.5) / WINDOW - 0.5) * (math.pi / 2)
    slopes = jnp.tan(angle_rad)
    path_len = 1.0 / jnp.cos(angle_rad)
    shift = x_pos[None, :] * slopes[:, None]
    start = jnp.floor(shift)
    fraction = shift - start
    lanes = jnp.arange(128)[None, None, :]
    info = jnp.zeros((mine, depth, 128), F32)
    columns = (
        start,
        fraction,
        jnp.broadcast_to(path_len[:, None], start.shape),
        jnp.mod(-start, float(width)),
        jnp.mod(start, float(width)),
    )
    for lane, column in enumerate(columns):
        info = jnp.where(lanes == lane, column[:, :, None], info)

    maps = jnp.transpose(element_maps[:, 0], (1, 0, 2))
    vmem = pl.BlockSpec(memory_space=pltpu.VMEM)
    plane = beams * heights
    updated, residual = pl.pallas_call(
        functools.partial(kernel, (beams, heights, groups)),
        out_shape=(
            jax.ShapeDtypeStruct((depth, elems, width), F32),
            jax.ShapeDtypeStruct((mine, elems, width), F32),
        ),
        in_specs=[vmem] * 10,
        out_specs=(vmem, vmem),
        scratch_shapes=[
            pltpu.VMEM((depth, elems, width), F32),
            pltpu.VMEM((total_angles, depth, 128), F32),
            pltpu.VMEM((total_angles, elems, width), F32),
            pltpu.SMEM((total_angles, depth, 128), F32),
            pltpu.VMEM((total_angles, depth, width), F32),
            pltpu.VMEM((total_angles, depth, width), F32),
            pltpu.VMEM((total_angles, depth * elems, width), F32),
            pltpu.VMEM((total_angles, depth * elems, width), F32),
            pltpu.VMEM((ITERS, beams, total_angles, elems + 8, width), F32),
            pltpu.VMEM((total_angles, elems, width), F32),
            pltpu.VMEM((depth, elems, width), F32),
            pltpu.VMEM((depth, elems, width), F32),
            pltpu.VMEM((ITERS, plane, 8, 128), F32),
            pltpu.SemaphoreType.DMA,
            pltpu.SemaphoreType.DMA((groups,)),
            pltpu.SemaphoreType.DMA((groups,)),
            pltpu.SemaphoreType.DMA((groups,)),
            pltpu.SemaphoreType.DMA((groups,)),
            pltpu.SemaphoreType.DMA((ITERS, beams, total_angles)),
            pltpu.SemaphoreType.DMA((ITERS, beams, total_angles)),
            pltpu.SemaphoreType.DMA((ITERS, plane)),
            pltpu.SemaphoreType.DMA((ITERS, plane)),
        ],
        compiler_params=pltpu.CompilerParams(
            collective_id=0, has_side_effects=True, vmem_limit_bytes=40 * 1024 * 1024
        ),
    )(
        maps, info, measured[:, :, 0], jnp.broadcast_to(absorb_incident[:, None], (elems, width)),
        out_high, out_low, back_high, back_low, exit_sum.astype(BF16), exit_sum.T.astype(BF16),
    )
    return (jnp.transpose(updated, (1, 0, 2))[:, None], residual[:, :, None])


def solution(mesh):
    in_specs = (
        P(None, "height", "beam", None),
        P("angles"),
        P(),
        P(),
        P(),
        P("angles", None, "height", None),
    )
    out_specs = (P(None, "height", "beam", None), P("angles", None, "height", None))
    return jax.shard_map(shards, mesh=mesh, in_specs=in_specs, out_specs=out_specs, check_vma=False)
```

```python
import functools
import math

import jax
import jax.numpy as jnp
from jax import lax
from jax.experimental import pallas as pl
from jax.experimental.pallas import tpu as pltpu
from jax.sharding import PartitionSpec as P

WINDOW = 96
ITERS = 2
EPSILON = 1e-06
STEP_SIZE = 0.05
DETECT_SCALE = 1.0 / 32.0
HIGHEST = lax.Precision.HIGHEST
MESH = pl.DeviceIdType.MESH
F32 = jnp.float32
BF16 = jnp.bfloat16
GROUP = 8


def split(value):
    high = value.astype(BF16)
    return high, (value - high.astype(F32)).astype(BF16)


def dot(left, right):
    return jnp.dot(left, right, preferred_element_type=F32)


def mix(high_ref, low_ref, value):
    high, low = split(value)
    return dot(high_ref[...], high) + (dot(low_ref[...], high) + dot(high_ref[...], low))


def mix_once(table_ref, value):
    return dot(table_ref[...], value.astype(BF16))


def spread_once(value, sums):
    return dot(value.astype(BF16), sums)


def tile_blocks(table, rows, elems):
    lane = lax.broadcasted_iota(jnp.int32, (elems, rows), 1)
    row = lax.broadcasted_iota(jnp.int32, (elems, rows), 0)
    repeat = jnp.zeros((elems, rows), F32)
    for block in range(GROUP):
        repeat = jnp.where(lane == row + block * elems, 1.0, repeat)
    tiled = dot(table, repeat.astype(BF16))
    lane = lax.broadcasted_iota(jnp.int32, tiled.shape, 1)
    bodies = [
        jnp.where((lane >= block * elems) & (lane < (block + 1) * elems), tiled, 0.0)[:elems]
        for block in range(GROUP)
    ]
    return tiled, bodies


def tail_rows(rows, elems, backward):
    lane = lax.broadcasted_iota(jnp.int32, (GROUP + 8, rows), 1)
    row = lax.broadcasted_iota(jnp.int32, (GROUP + 8, rows), 0)
    block = jnp.zeros((GROUP + 8, rows), jnp.int32)
    for step in range(1, GROUP):
        block = block + jnp.where(lane >= step * elems, 1, 0)
    ahead = block > row if backward else block < row
    weight = jnp.where(ahead, 1.0, jnp.where(block == row, 0.5, 0.0))
    return jnp.where(row < GROUP, weight, 1.0)


def spread(value, sums):
    high, low = split(value)
    return dot(high, sums) + dot(low, sums)


def kernel(
    sizes,
    maps_ref, info_ref, measured_ref, incident_ref, table_ref, turned_ref,
    current, residual_ref,
    shifted, info, seen, scalars, coef0, coef1, sampled, fading, slabs, misfit,
    acc0, acc1, squares, out_high, out_low, back_high, exit_ref, enter_ref,
    local_sem, info_send, info_recv, seen_send, seen_recv,
    slab_send, slab_recv, norm_send, norm_recv,
):
    beams, heights, groups = sizes
    elems, width = maps_ref.shape[1:]
    depth = maps_ref.shape[0]
    mine = info_ref.shape[0]
    total_angles = groups * mine
    xgroups = depth // GROUP
    rows = GROUP * elems
    beam = lax.axis_index("beam")
    height = lax.axis_index("height")
    group = lax.axis_index("angles")
    plane = beams * heights
    place = beam * heights + height
    cells = float(elems * depth * width * plane)

    def plane_id(index):
        return (index // heights, lax.rem(index, heights), group)

    barrier = pltpu.get_barrier_semaphore()
    for step in range(1, groups):
        pl.semaphore_signal(
            barrier, inc=1, device_id=(beam, height, lax.rem(group + step, groups)), device_id_type=MESH
        )

    @pl.loop(1, plane)
    def _(step):
        pl.semaphore_signal(
            barrier, inc=1, device_id=plane_id(lax.rem(place + step, plane)), device_id_type=MESH
        )

    pl.semaphore_wait(barrier, groups - 1 + plane - 1)

    def info_copy(step, slot):
        peer = lax.rem(group + step, groups)
        part = pl.ds(slot * mine, mine)
        return pltpu.make_async_remote_copy(
            info_ref, info.at[part], info_send.at[peer], info_recv.at[slot],
            device_id=(beam, height, peer), device_id_type=MESH,
        )

    def seen_copy(step, slot):
        peer = lax.rem(group + step, groups)
        part = pl.ds(slot * mine, mine)
        return pltpu.make_async_remote_copy(
            measured_ref, seen.at[part], seen_send.at[peer], seen_recv.at[slot],
            device_id=(beam, height, peer), device_id_type=MESH,
        )

    for step in range(1, groups):
        info_copy(step, group).start()
    for step in range(1, groups):
        seen_copy(step, group).start()
    info[pl.ds(group * mine, mine)] = info_ref[...]
    seen[pl.ds(group * mine, mine)] = measured_ref[...]

    tail = tail_rows(rows, elems, False)
    for part, out_ref in zip(split(table_ref[...]), (out_high, out_low)):
        tiled, bodies = tile_blocks(part, rows, elems)
        incident_rows = jnp.concatenate([tiled[elems:]] * ((GROUP + 8) // 8), axis=0)
        out_ref[...] = jnp.concatenate(bodies + [tail * incident_rows], axis=0).astype(BF16)
    _, bodies = tile_blocks(turned_ref[...].astype(BF16), rows, elems)
    back_high[...] = jnp.concatenate(bodies + [tail_rows(rows, elems, True)], axis=0).astype(BF16)
    source_at = lax.broadcasted_iota(jnp.int32, (width, width), 0)
    exit_at = lax.broadcasted_iota(jnp.int32, (width, width), 1)
    half = jnp.where(source_at == exit_at, 0.5, 0.0)
    exit_ref[...] = jnp.where(source_at > exit_at, 1.0, half).astype(BF16)
    enter_ref[...] = jnp.where(source_at < exit_at, 1.0, half).astype(BF16)
    for x in range(depth):
        plane_x = maps_ref[x]
        current[x] = plane_x
        shifted[x] = pltpu.roll(plane_x, width - 1, 1)

    for step in range(1, groups):
        copy = info_copy(step, lax.rem(group + step, groups))
        copy.wait_send()
        copy.wait_recv()
    fill = pltpu.make_async_copy(info, scalars, local_sem)
    fill.start()
    fill.wait()

    def slab_copy(iteration, a, step, slot):
        peer = lax.rem(beam + step, beams)
        return pltpu.make_async_remote_copy(
            slabs.at[iteration, beam, a], slabs.at[iteration, slot, a],
            slab_send.at[iteration, peer, a], slab_recv.at[iteration, slot, a],
            device_id=(peer, height, group), device_id_type=MESH,
        )

    def norm_copy(iteration, step, slot):
        peer = lax.rem(place + step, plane)
        return pltpu.make_async_remote_copy(
            squares.at[iteration, place], squares.at[iteration, slot],
            norm_send.at[iteration, peer], norm_recv.at[iteration, slot],
            device_id=plane_id(peer), device_id_type=MESH,
        )

    def forward(iteration, a):
        cols = info[a]
        start = jnp.broadcast_to(cols[:, 0:1], (depth, width))
        fraction = cols[:, 1:2]
        path = cols[0:1, 2:3]
        position = lax.broadcasted_iota(jnp.int32, (depth, width), 1).astype(F32)
        below = start < 0
        inside = (below & (position <= (width - 1) + start)) | (~below & (position >= start))
        edge = below & (position == width - 1) & (start >= -width)
        inner = inside & (position <= width - 2)
        coef0[a] = jnp.where(inside, 1.0 - fraction, 0.0)
        coef1[a] = jnp.where(inner | edge, fraction, 0.0)
        carry = jnp.zeros((1, width), F32)
        total = jnp.zeros((elems, width), F32)
        for g in range(xgroups):
            for xi in range(GROUP):
                x = g * GROUP + xi
                blend = coef0[a, x : x + 1] * current[x] + coef1[a, x : x + 1] * shifted[x]
                shift = scalars[a, x, 3].astype(jnp.int32)
                sampled[a, x * elems : (x + 1) * elems] = pltpu.roll(blend, shift, 1)
            mu = mix(out_high, out_low, sampled[a, g * rows : (g + 1) * rows])
            depth_in = path * mu[rows : rows + GROUP] + carry
            carry = carry + path * mu[rows + GROUP : rows + GROUP + 1]
            tau = spread(mu[:rows], exit_ref[...])
            for xi in range(GROUP):
                x = g * GROUP + xi
                fade = jnp.exp(-(tau[xi * elems : (xi + 1) * elems] + depth_in[xi : xi + 1]))
                fading[a, x * elems : (x + 1) * elems] = fade
                total = total + fade * sampled[a, x * elems : (x + 1) * elems]
        slabs[iteration, beam, a, 0:elems] = (path * DETECT_SCALE) * total
        slabs[iteration, beam, a, elems : elems + 8] = jnp.broadcast_to(carry, (8, width))
        for step in range(1, beams):
            slab_copy(iteration, a, step, beam).start()

    def backward(iteration, a):
        for step in range(1, beams):
            copy = slab_copy(iteration, a, step, lax.rem(beam + step, beams))
            copy.wait_send()
            copy.wait_recv()
        cols = info[a]
        path = cols[0:1, 2:3]
        before = jnp.zeros((1, width), F32)
        scale = jnp.zeros((1, width), F32)
        fluor = jnp.zeros((elems, width), F32)
        after = jnp.zeros((elems, width), F32)
        for b in range(beams):
            dim = jnp.exp(-before)
            part = dim * slabs[iteration, b, a, 0:elems]
            fluor = fluor + part
            after = after + jnp.where(b > beam, 1.0, 0.0) * part
            scale = scale + jnp.where(b == beam, 1.0, 0.0) * dim
            before = before + slabs[iteration, b, a, elems : elems + 1]
        residual = fluor - seen[a]
        misfit[a] = residual
        carry = jnp.sum(residual * after, axis=0, keepdims=True)
        source = residual * (scale * (path * DETECT_SCALE))
        incident = path * incident_ref[...]
        for g in reversed(range(xgroups)):
            emitted = []
            for xi in range(GROUP):
                x = g * GROUP + xi
                part = slice(x * elems, (x + 1) * elems)
                emitted.append(source * fading[a, part] * sampled[a, part])
            mixed = mix_once(back_high, jnp.concatenate(emitted, axis=0))
            behind = mixed[rows : rows + GROUP] + carry
            carry = carry + mixed[rows + GROUP : rows + GROUP + 1]
            back = spread_once(mixed[:rows], enter_ref[...])
            for xi in range(GROUP):
                x = g * GROUP + xi
                weighted = source * fading[a, x * elems : (x + 1) * elems]
                grad = (
                    weighted
                    - incident * behind[xi : xi + 1]
                    - back[xi * elems : (xi + 1) * elems]
                )
                shift = scalars[a, x, 4].astype(jnp.int32)
                grad = pltpu.roll(grad, shift, 1)
                acc0[x] = acc0[x] + coef0[a, x : x + 1] * grad
                acc1[x] = acc1[x] + coef1[a, x : x + 1] * grad

    @pl.loop(0, ITERS)
    def _(iteration):
        @pl.loop(0, total_angles)
        def _(a):
            forward(iteration, a)

        @pl.when(iteration == 0)
        def _():
            for step in range(1, groups):
                copy = seen_copy(step, lax.rem(group + step, groups))
                copy.wait_send()
                copy.wait_recv()

        acc0[...] = jnp.zeros_like(acc0)
        acc1[...] = jnp.zeros_like(acc1)

        @pl.loop(0, total_angles)
        def _(a):
            backward(iteration, a)

        square = jnp.zeros((8, width), F32)
        for x in range(depth):
            grad = acc0[x] + pltpu.roll(acc1[x], 1, 1)
            acc0[x] = grad
            grad = grad * grad
            for row in range(0, elems, 8):
                square = square + grad[row : row + 8]
        folded = square[:, 0:128]
        for lane in range(128, width, 128):
            folded = folded + square[:, lane : lane + 128]
        squares[iteration, place] = folded

        @pl.loop(1, plane)
        def _(step):
            norm_copy(iteration, step, place).start()

        @pl.loop(1, plane)
        def _(step):
            copy = norm_copy(iteration, step, lax.rem(place + step, plane))
            copy.wait_send()
            copy.wait_recv()

        whole = jnp.sum(squares[iteration], axis=0)
        whole = jnp.sum(jnp.sum(whole, axis=0, keepdims=True), axis=1, keepdims=True)
        rate = STEP_SIZE / jnp.sqrt(whole / cells + EPSILON)
        for x in range(depth):
            plane_x = current[x] - rate * acc0[x]
            current[x] = plane_x
            shifted[x] = pltpu.roll(plane_x, width - 1, 1)

    residual_ref[...] = misfit[pl.ds(group * mine, mine)]


def shards(element_maps, angles, absorb_incident, absorb_table, line_index, measured):
    elems, height_rows, depth, width = element_maps.shape
    beams = lax.axis_size("beam")
    heights = lax.axis_size("height")
    groups = lax.axis_size("angles")
    mine = angles.shape[0]
    total_angles = groups * mine
    line_total = depth * beams
    rows = GROUP * elems

    pick_line = (line_index[:, None] == jnp.arange(absorb_table.shape[0])[None, :]).astype(F32)
    absorb_out = jnp.dot(pick_line, absorb_table, precision=HIGHEST)
    table = jnp.concatenate(
        [absorb_out, jnp.broadcast_to(absorb_incident[None, :], (8, elems))], axis=0
    )
    x_pos = (lax.axis_index("beam") * depth + jnp.arange(depth)).astype(F32) - (line_total - 1) / 2
    angle_rad = ((angles.astype(F32) + 0.5) / WINDOW - 0.5) * (math.pi / 2)
    slopes = jnp.tan(angle_rad)
    path_len = 1.0 / jnp.cos(angle_rad)
    shift = x_pos[None, :] * slopes[:, None]
    start = jnp.floor(shift)
    fraction = shift - start
    lanes = jnp.arange(128)[None, None, :]
    info = jnp.zeros((mine, depth, 128), F32)
    columns = (
        start,
        fraction,
        jnp.broadcast_to(path_len[:, None], start.shape),
        jnp.mod(-start, float(width)),
        jnp.mod(start, float(width)),
    )
    for lane, column in enumerate(columns):
        info = jnp.where(lanes == lane, column[:, :, None], info)

    maps = jnp.transpose(element_maps[:, 0], (1, 0, 2))
    vmem = pl.BlockSpec(memory_space=pltpu.VMEM)
    plane = beams * heights
    updated, residual = pl.pallas_call(
        functools.partial(kernel, (beams, heights, groups)),
        out_shape=(
            jax.ShapeDtypeStruct((depth, elems, width), F32),
            jax.ShapeDtypeStruct((mine, elems, width), F32),
        ),
        in_specs=[vmem] * 6,
        out_specs=(vmem, vmem),
        scratch_shapes=[
            pltpu.VMEM((depth, elems, width), F32),
            pltpu.VMEM((total_angles, depth, 128), F32),
            pltpu.VMEM((total_angles, elems, width), F32),
            pltpu.SMEM((total_angles, depth, 128), F32),
            pltpu.VMEM((total_angles, depth, width), F32),
            pltpu.VMEM((total_angles, depth, width), F32),
            pltpu.VMEM((total_angles, depth * elems, width), F32),
            pltpu.VMEM((total_angles, depth * elems, width), F32),
            pltpu.VMEM((ITERS, beams, total_angles, elems + 8, width), F32),
            pltpu.VMEM((total_angles, elems, width), F32),
            pltpu.VMEM((depth, elems, width), F32),
            pltpu.VMEM((depth, elems, width), F32),
            pltpu.VMEM((ITERS, plane, 8, 128), F32),
            pltpu.VMEM((rows + GROUP + 8, rows), BF16),
            pltpu.VMEM((rows + GROUP + 8, rows), BF16),
            pltpu.VMEM((rows + GROUP + 8, rows), BF16),
            pltpu.VMEM((width, width), BF16),
            pltpu.VMEM((width, width), BF16),
            pltpu.SemaphoreType.DMA,
            pltpu.SemaphoreType.DMA((groups,)),
            pltpu.SemaphoreType.DMA((groups,)),
            pltpu.SemaphoreType.DMA((groups,)),
            pltpu.SemaphoreType.DMA((groups,)),
            pltpu.SemaphoreType.DMA((ITERS, beams, total_angles)),
            pltpu.SemaphoreType.DMA((ITERS, beams, total_angles)),
            pltpu.SemaphoreType.DMA((ITERS, plane)),
            pltpu.SemaphoreType.DMA((ITERS, plane)),
        ],
        compiler_params=pltpu.CompilerParams(
            collective_id=0, has_side_effects=True, vmem_limit_bytes=40 * 1024 * 1024
        ),
    )(
        maps, info, measured[:, :, 0], jnp.broadcast_to(absorb_incident[:, None], (elems, width)),
        table, absorb_out.T,
    )
    return (jnp.transpose(updated, (1, 0, 2))[:, None], residual[:, :, None])


def solution(mesh):
    in_specs = (
        P(None, "height", "beam", None),
        P("angles"),
        P(),
        P(),
        P(),
        P("angles", None, "height", None),
    )
    out_specs = (P(None, "height", "beam", None), P("angles", None, "height", None))
    return jax.shard_map(shards, mesh=mesh, in_specs=in_specs, out_specs=out_specs, check_vma=False)
```

```python
import functools
import math

import jax
import jax.numpy as jnp
from jax import lax
from jax.experimental import pallas as pl
from jax.experimental.pallas import tpu as pltpu
from jax.sharding import PartitionSpec as P

WINDOW = 96
ITERS = 2
EPSILON = 1e-06
STEP_SIZE = 0.05
DETECT_SCALE = 1.0 / 32.0
HIGHEST = lax.Precision.HIGHEST
MESH = pl.DeviceIdType.MESH
F32 = jnp.float32
BF16 = jnp.bfloat16
GROUP = 8


def split(value):
    high = value.astype(BF16)
    return high, (value - high.astype(F32)).astype(BF16)


def dot(left, right):
    return jnp.dot(left, right, preferred_element_type=F32)


def mix(high_ref, low_ref, value):
    high, low = split(value)
    return dot(high_ref[...], high) + (dot(low_ref[...], high) + dot(high_ref[...], low))


def mix_once(table_ref, value):
    return dot(table_ref[...], value.astype(BF16))


def spread_once(value, sums):
    return dot(value.astype(BF16), sums)


def tile_blocks(table, rows, elems):
    lane = lax.broadcasted_iota(jnp.int32, (elems, rows), 1)
    row = lax.broadcasted_iota(jnp.int32, (elems, rows), 0)
    repeat = jnp.zeros((elems, rows), F32)
    for block in range(GROUP):
        repeat = jnp.where(lane == row + block * elems, 1.0, repeat)
    tiled = dot(table, repeat.astype(BF16))
    lane = lax.broadcasted_iota(jnp.int32, tiled.shape, 1)
    bodies = [
        jnp.where((lane >= block * elems) & (lane < (block + 1) * elems), tiled, 0.0)[:elems]
        for block in range(GROUP)
    ]
    return tiled, bodies


def tail_rows(rows, elems, backward):
    lane = lax.broadcasted_iota(jnp.int32, (GROUP + 8, rows), 1)
    row = lax.broadcasted_iota(jnp.int32, (GROUP + 8, rows), 0)
    block = jnp.zeros((GROUP + 8, rows), jnp.int32)
    for step in range(1, GROUP):
        block = block + jnp.where(lane >= step * elems, 1, 0)
    ahead = block > row if backward else block < row
    weight = jnp.where(ahead, 1.0, jnp.where(block == row, 0.5, 0.0))
    return jnp.where(row < GROUP, weight, 1.0)


def spread(value, sums):
    high, low = split(value)
    return dot(high, sums) + dot(low, sums)


def kernel(
    sizes,
    maps_ref, info_ref, measured_ref, incident_ref, table_ref, turned_ref,
    current, residual_ref,
    shifted, info, seen, scalars, coef0, coef1, sampled, fading, slabs, misfit,
    acc0, acc1, squares, out_high, out_low, back_high, exit_ref, enter_ref,
    local_sem, maps_sem, info_send, info_recv, seen_send, seen_recv,
    slab_send, slab_recv, norm_send, norm_recv,
):
    beams, heights, groups = sizes
    elems, depth, width = maps_ref.shape
    mine = info_ref.shape[0]
    total_angles = groups * mine
    xgroups = depth // GROUP
    pairs = math.gcd(total_angles, 2)
    rows = GROUP * elems
    beam = lax.axis_index("beam")
    height = lax.axis_index("height")
    group = lax.axis_index("angles")
    plane = beams * heights
    place = beam * heights + height
    cells = float(elems * depth * width * plane)

    def plane_id(index):
        return (index // heights, lax.rem(index, heights), group)

    barrier = pltpu.get_barrier_semaphore()
    for step in range(1, groups):
        pl.semaphore_signal(
            barrier, inc=1, device_id=(beam, height, lax.rem(group + step, groups)), device_id_type=MESH
        )

    @pl.loop(1, plane)
    def _(step):
        pl.semaphore_signal(
            barrier, inc=1, device_id=plane_id(lax.rem(place + step, plane)), device_id_type=MESH
        )

    pl.semaphore_wait(barrier, groups - 1 + plane - 1)

    def info_copy(step, slot):
        peer = lax.rem(group + step, groups)
        part = pl.ds(slot * mine, mine)
        return pltpu.make_async_remote_copy(
            info_ref, info.at[part], info_send.at[peer], info_recv.at[slot],
            device_id=(beam, height, peer), device_id_type=MESH,
        )

    def seen_copy(step, slot):
        peer = lax.rem(group + step, groups)
        part = pl.ds(slot * mine, mine)
        return pltpu.make_async_remote_copy(
            measured_ref, seen.at[part], seen_send.at[peer], seen_recv.at[slot],
            device_id=(beam, height, peer), device_id_type=MESH,
        )

    for step in range(1, groups):
        info_copy(step, group).start()
    for step in range(1, groups):
        seen_copy(step, group).start()
    info[pl.ds(group * mine, mine)] = info_ref[...]
    seen[pl.ds(group * mine, mine)] = measured_ref[...]

    fetches = [
        pltpu.make_async_copy(maps_ref.at[:, x], current.at[x], maps_sem.at[x]) for x in range(depth)
    ]
    for fetch in fetches:
        fetch.start()
    tail = tail_rows(rows, elems, False)
    for part, out_ref in zip(split(table_ref[...]), (out_high, out_low)):
        tiled, bodies = tile_blocks(part, rows, elems)
        incident_rows = jnp.concatenate([tiled[elems:]] * ((GROUP + 8) // 8), axis=0)
        out_ref[...] = jnp.concatenate(bodies + [tail * incident_rows], axis=0).astype(BF16)
    _, bodies = tile_blocks(turned_ref[...].astype(BF16), rows, elems)
    back_high[...] = jnp.concatenate(bodies + [tail_rows(rows, elems, True)], axis=0).astype(BF16)
    source_at = lax.broadcasted_iota(jnp.int32, (width, width), 0)
    exit_at = lax.broadcasted_iota(jnp.int32, (width, width), 1)
    half = jnp.where(source_at == exit_at, 0.5, 0.0)
    exit_ref[...] = jnp.where(source_at > exit_at, 1.0, half).astype(BF16)
    enter_ref[...] = jnp.where(source_at < exit_at, 1.0, half).astype(BF16)
    for x in range(depth):
        fetches[x].wait()
        shifted[x] = pltpu.roll(current[x], width - 1, 1)

    for step in range(1, groups):
        copy = info_copy(step, lax.rem(group + step, groups))
        copy.wait_send()
        copy.wait_recv()
    fill = pltpu.make_async_copy(info, scalars, local_sem)
    fill.start()
    fill.wait()

    def slab_copy(iteration, a, step, slot):
        peer = lax.rem(beam + step, beams)
        return pltpu.make_async_remote_copy(
            slabs.at[iteration, beam, a], slabs.at[iteration, slot, a],
            slab_send.at[iteration, peer, a], slab_recv.at[iteration, slot, a],
            device_id=(peer, height, group), device_id_type=MESH,
        )

    def norm_copy(iteration, step, slot):
        peer = lax.rem(place + step, plane)
        return pltpu.make_async_remote_copy(
            squares.at[iteration, place], squares.at[iteration, slot],
            norm_send.at[iteration, peer], norm_recv.at[iteration, slot],
            device_id=plane_id(peer), device_id_type=MESH,
        )

    def forward(iteration, a):
        cols = info[a]
        start = jnp.broadcast_to(cols[:, 0:1], (depth, width))
        fraction = cols[:, 1:2]
        path = cols[0:1, 2:3]
        position = lax.broadcasted_iota(jnp.int32, (depth, width), 1).astype(F32)
        below = start < 0
        inside = (below & (position <= (width - 1) + start)) | (~below & (position >= start))
        edge = below & (position == width - 1) & (start >= -width)
        inner = inside & (position <= width - 2)
        coef0[a] = jnp.where(inside, 1.0 - fraction, 0.0)
        coef1[a] = jnp.where(inner | edge, fraction, 0.0)
        for x in range(depth):
            blend = coef0[a, x : x + 1] * current[x] + coef1[a, x : x + 1] * shifted[x]
            shift = scalars[a, x, 3].astype(jnp.int32)
            sampled[a, x * elems : (x + 1) * elems] = pltpu.roll(blend, shift, 1)
        return path

    def forward_pair(iteration, pair):
        paths = [forward(iteration, a) for a in pair]
        carries = [jnp.zeros((1, width), F32) for _ in pair]
        totals = [jnp.zeros((elems, width), F32) for _ in pair]
        for g in range(xgroups):
            depths = []
            for n, a in enumerate(pair):
                mu = mix(out_high, out_low, sampled[a, g * rows : (g + 1) * rows])
                depth_in = paths[n] * mu[rows : rows + GROUP] + carries[n]
                carries[n] = carries[n] + paths[n] * mu[rows + GROUP : rows + GROUP + 1]
                depths.append((depth_in, spread(mu[:rows], exit_ref[...])))
            for n, a in enumerate(pair):
                depth_in, tau = depths[n]
                for xi in range(GROUP):
                    part = slice((g * GROUP + xi) * elems, (g * GROUP + xi + 1) * elems)
                    fade = jnp.exp(-(tau[xi * elems : (xi + 1) * elems] + depth_in[xi : xi + 1]))
                    fading[a, part] = fade
                    totals[n] = totals[n] + fade * sampled[a, part]
        for n, a in enumerate(pair):
            slabs[iteration, beam, a, 0:elems] = (paths[n] * DETECT_SCALE) * totals[n]
            slabs[iteration, beam, a, elems : elems + 8] = jnp.broadcast_to(carries[n], (8, width))
            for step in range(1, beams):
                slab_copy(iteration, a, step, beam).start()

    def backward(iteration, a):
        for step in range(1, beams):
            copy = slab_copy(iteration, a, step, lax.rem(beam + step, beams))
            copy.wait_send()
            copy.wait_recv()
        cols = info[a]
        path = cols[0:1, 2:3]
        before = jnp.zeros((1, width), F32)
        scale = jnp.zeros((1, width), F32)
        fluor = jnp.zeros((elems, width), F32)
        after = jnp.zeros((elems, width), F32)
        for b in range(beams):
            dim = jnp.exp(-before)
            part = dim * slabs[iteration, b, a, 0:elems]
            fluor = fluor + part
            after = after + jnp.where(b > beam, 1.0, 0.0) * part
            scale = scale + jnp.where(b == beam, 1.0, 0.0) * dim
            before = before + slabs[iteration, b, a, elems : elems + 1]
        residual = fluor - seen[a]
        misfit[a] = residual
        carry = jnp.sum(residual * after, axis=0, keepdims=True)
        source = residual * (scale * (path * DETECT_SCALE))
        incident = path * incident_ref[...]
        return source, incident, carry

    def backward_pair(iteration, pair):
        heads = [backward(iteration, a) for a in pair]
        carries = [head[2] for head in heads]
        for g in reversed(range(xgroups)):
            sensed = []
            for n, a in enumerate(pair):
                source = heads[n][0]
                emitted = []
                for xi in range(GROUP):
                    x = g * GROUP + xi
                    part = slice(x * elems, (x + 1) * elems)
                    emitted.append(source * fading[a, part] * sampled[a, part])
                mixed = mix_once(back_high, jnp.concatenate(emitted, axis=0))
                behind = mixed[rows : rows + GROUP] + carries[n]
                carries[n] = carries[n] + mixed[rows + GROUP : rows + GROUP + 1]
                sensed.append((behind, spread_once(mixed[:rows], enter_ref[...])))
            for xi in range(GROUP):
                x = g * GROUP + xi
                sum0, sum1 = acc0[x], acc1[x]
                for n, a in enumerate(pair):
                    source, incident, _ = heads[n]
                    behind, back = sensed[n]
                    grad = (
                        source * fading[a, x * elems : (x + 1) * elems]
                        - incident * behind[xi : xi + 1]
                        - back[xi * elems : (xi + 1) * elems]
                    )
                    grad = pltpu.roll(grad, scalars[a, x, 4].astype(jnp.int32), 1)
                    sum0 = sum0 + coef0[a, x : x + 1] * grad
                    sum1 = sum1 + coef1[a, x : x + 1] * grad
                acc0[x] = sum0
                acc1[x] = sum1

    @pl.loop(0, ITERS)
    def _(iteration):
        @pl.loop(0, total_angles // pairs)
        def _(step):
            forward_pair(iteration, [step * pairs + n for n in range(pairs)])

        @pl.when(iteration == 0)
        def _():
            for step in range(1, groups):
                copy = seen_copy(step, lax.rem(group + step, groups))
                copy.wait_send()
                copy.wait_recv()

        acc0[...] = jnp.zeros_like(acc0)
        acc1[...] = jnp.zeros_like(acc1)

        @pl.loop(0, total_angles // pairs)
        def _(step):
            backward_pair(iteration, [step * pairs + n for n in range(pairs)])

        square = jnp.zeros((8, width), F32)
        for x in range(depth):
            grad = acc0[x] + pltpu.roll(acc1[x], 1, 1)
            acc0[x] = grad
            grad = grad * grad
            for row in range(0, elems, 8):
                square = square + grad[row : row + 8]
        folded = square[:, 0:128]
        for lane in range(128, width, 128):
            folded = folded + square[:, lane : lane + 128]
        squares[iteration, place] = folded

        @pl.loop(1, plane)
        def _(step):
            norm_copy(iteration, step, place).start()

        @pl.loop(1, plane)
        def _(step):
            copy = norm_copy(iteration, step, lax.rem(place + step, plane))
            copy.wait_send()
            copy.wait_recv()

        whole = jnp.sum(squares[iteration], axis=0)
        whole = jnp.sum(jnp.sum(whole, axis=0, keepdims=True), axis=1, keepdims=True)
        rate = STEP_SIZE / jnp.sqrt(whole / cells + EPSILON)
        for x in range(depth):
            plane_x = current[x] - rate * acc0[x]
            current[x] = plane_x
            shifted[x] = pltpu.roll(plane_x, width - 1, 1)

    residual_ref[...] = misfit[pl.ds(group * mine, mine)]


def shards(element_maps, angles, absorb_incident, absorb_table, line_index, measured):
    elems, height_rows, depth, width = element_maps.shape
    beams = lax.axis_size("beam")
    heights = lax.axis_size("height")
    groups = lax.axis_size("angles")
    mine = angles.shape[0]
    total_angles = groups * mine
    line_total = depth * beams
    rows = GROUP * elems

    pick_line = (line_index[:, None] == jnp.arange(absorb_table.shape[0])[None, :]).astype(F32)
    absorb_out = jnp.dot(pick_line, absorb_table, precision=HIGHEST)
    table = jnp.concatenate(
        [absorb_out, jnp.broadcast_to(absorb_incident[None, :], (8, elems))], axis=0
    )
    x_pos = (lax.axis_index("beam") * depth + jnp.arange(depth)).astype(F32) - (line_total - 1) / 2
    angle_rad = ((angles.astype(F32) + 0.5) / WINDOW - 0.5) * (math.pi / 2)
    slopes = jnp.tan(angle_rad)
    path_len = 1.0 / jnp.cos(angle_rad)
    shift = x_pos[None, :] * slopes[:, None]
    start = jnp.floor(shift)
    fraction = shift - start
    lanes = jnp.arange(128)[None, None, :]
    info = jnp.zeros((mine, depth, 128), F32)
    columns = (
        start,
        fraction,
        jnp.broadcast_to(path_len[:, None], start.shape),
        jnp.mod(-start, float(width)),
        jnp.mod(start, float(width)),
    )
    for lane, column in enumerate(columns):
        info = jnp.where(lanes == lane, column[:, :, None], info)

    maps = element_maps[:, 0]
    vmem = pl.BlockSpec(memory_space=pltpu.VMEM)
    plane = beams * heights
    updated, residual = pl.pallas_call(
        functools.partial(kernel, (beams, heights, groups)),
        out_shape=(
            jax.ShapeDtypeStruct((depth, elems, width), F32),
            jax.ShapeDtypeStruct((mine, elems, width), F32),
        ),
        in_specs=[pl.BlockSpec(memory_space=pl.ANY)] + [vmem] * 5,
        out_specs=(vmem, vmem),
        scratch_shapes=[
            pltpu.VMEM((depth, elems, width), F32),
            pltpu.VMEM((total_angles, depth, 128), F32),
            pltpu.VMEM((total_angles, elems, width), F32),
            pltpu.SMEM((total_angles, depth, 128), F32),
            pltpu.VMEM((total_angles, depth, width), F32),
            pltpu.VMEM((total_angles, depth, width), F32),
            pltpu.VMEM((total_angles, depth * elems, width), F32),
            pltpu.VMEM((total_angles, depth * elems, width), F32),
            pltpu.VMEM((ITERS, beams, total_angles, elems + 8, width), F32),
            pltpu.VMEM((total_angles, elems, width), F32),
            pltpu.VMEM((depth, elems, width), F32),
            pltpu.VMEM((depth, elems, width), F32),
            pltpu.VMEM((ITERS, plane, 8, 128), F32),
            pltpu.VMEM((rows + GROUP + 8, rows), BF16),
            pltpu.VMEM((rows + GROUP + 8, rows), BF16),
            pltpu.VMEM((rows + GROUP + 8, rows), BF16),
            pltpu.VMEM((width, width), BF16),
            pltpu.VMEM((width, width), BF16),
            pltpu.SemaphoreType.DMA,
            pltpu.SemaphoreType.DMA((depth,)),
            pltpu.SemaphoreType.DMA((groups,)),
            pltpu.SemaphoreType.DMA((groups,)),
            pltpu.SemaphoreType.DMA((groups,)),
            pltpu.SemaphoreType.DMA((groups,)),
            pltpu.SemaphoreType.DMA((ITERS, beams, total_angles)),
            pltpu.SemaphoreType.DMA((ITERS, beams, total_angles)),
            pltpu.SemaphoreType.DMA((ITERS, plane)),
            pltpu.SemaphoreType.DMA((ITERS, plane)),
        ],
        compiler_params=pltpu.CompilerParams(
            collective_id=0, has_side_effects=True, vmem_limit_bytes=40 * 1024 * 1024
        ),
    )(
        maps, info, measured[:, :, 0], jnp.broadcast_to(absorb_incident[:, None], (elems, width)),
        table, absorb_out.T,
    )
    return (jnp.transpose(updated, (1, 0, 2))[:, None], residual[:, :, None])


def solution(mesh):
    in_specs = (
        P(None, "height", "beam", None),
        P("angles"),
        P(),
        P(),
        P(),
        P("angles", None, "height", None),
    )
    out_specs = (P(None, "height", "beam", None), P("angles", None, "height", None))
    return jax.shard_map(shards, mesh=mesh, in_specs=in_specs, out_specs=out_specs, check_vma=False)
```

```python
import functools
import math

import jax
import jax.numpy as jnp
from jax import lax
from jax.experimental import pallas as pl
from jax.experimental.pallas import tpu as pltpu
from jax.sharding import PartitionSpec as P

WINDOW = 96
ITERS = 2
EPSILON = 1e-06
STEP_SIZE = 0.05
DETECT_SCALE = 1.0 / 32.0
HIGHEST = lax.Precision.HIGHEST
MESH = pl.DeviceIdType.MESH
F32 = jnp.float32
BF16 = jnp.bfloat16
GROUP = 8


def split(value):
    high = value.astype(BF16)
    return high, (value - high.astype(F32)).astype(BF16)


def dot(left, right):
    return jnp.dot(left, right, preferred_element_type=F32)


def mix(high_ref, low_ref, value):
    high, low = split(value)
    return dot(high_ref[...], high) + (dot(low_ref[...], high) + dot(high_ref[...], low))


def mix_once(table_ref, value):
    return dot(table_ref[...], value.astype(BF16))


def spread_once(value, sums):
    return dot(value.astype(BF16), sums)


def tile_blocks(table, rows, elems):
    lane = lax.broadcasted_iota(jnp.int32, (elems, rows), 1)
    row = lax.broadcasted_iota(jnp.int32, (elems, rows), 0)
    repeat = jnp.zeros((elems, rows), F32)
    for block in range(GROUP):
        repeat = jnp.where(lane == row + block * elems, 1.0, repeat)
    tiled = dot(table, repeat.astype(BF16))
    lane = lax.broadcasted_iota(jnp.int32, tiled.shape, 1)
    bodies = [
        jnp.where((lane >= block * elems) & (lane < (block + 1) * elems), tiled, 0.0)[:elems]
        for block in range(GROUP)
    ]
    return tiled, bodies


def tail_rows(rows, elems, backward):
    lane = lax.broadcasted_iota(jnp.int32, (GROUP + 8, rows), 1)
    row = lax.broadcasted_iota(jnp.int32, (GROUP + 8, rows), 0)
    block = jnp.zeros((GROUP + 8, rows), jnp.int32)
    for step in range(1, GROUP):
        block = block + jnp.where(lane >= step * elems, 1, 0)
    ahead = block > row if backward else block < row
    weight = jnp.where(ahead, 1.0, jnp.where(block == row, 0.5, 0.0))
    return jnp.where(row < GROUP, weight, 1.0)


def spread(value, sums):
    high, low = split(value)
    return dot(high, sums) + dot(low, sums)


def kernel(
    sizes,
    maps_ref, info_ref, measured_ref, incident_ref, table_ref, turned_ref,
    current, residual_ref,
    shifted, info, seen, scalars, coef0, coef1, sampled, fading, slabs, misfit,
    acc0, acc1, squares, out_high, out_low, back_high, exit_ref, enter_ref,
    local_sem, maps_sem, info_send, info_recv, seen_send, seen_recv,
    slab_send, slab_recv, norm_send, norm_recv,
):
    beams, heights, groups = sizes
    elems, depth, width = maps_ref.shape
    mine = info_ref.shape[0]
    total_angles = groups * mine
    xgroups = depth // GROUP
    pairs = math.gcd(total_angles, 4)
    rows = GROUP * elems
    beam = lax.axis_index("beam")
    height = lax.axis_index("height")
    group = lax.axis_index("angles")
    plane = beams * heights
    place = beam * heights + height
    cells = float(elems * depth * width * plane)

    def plane_id(index):
        return (index // heights, lax.rem(index, heights), group)

    barrier = pltpu.get_barrier_semaphore()
    for step in range(1, groups):
        pl.semaphore_signal(
            barrier, inc=1, device_id=(beam, height, lax.rem(group + step, groups)), device_id_type=MESH
        )

    @pl.loop(1, plane)
    def _(step):
        pl.semaphore_signal(
            barrier, inc=1, device_id=plane_id(lax.rem(place + step, plane)), device_id_type=MESH
        )

    pl.semaphore_wait(barrier, groups - 1 + plane - 1)

    def info_copy(step, slot):
        peer = lax.rem(group + step, groups)
        part = pl.ds(slot * mine, mine)
        return pltpu.make_async_remote_copy(
            info_ref, info.at[part], info_send.at[peer], info_recv.at[slot],
            device_id=(beam, height, peer), device_id_type=MESH,
        )

    def seen_copy(step, slot):
        peer = lax.rem(group + step, groups)
        part = pl.ds(slot * mine, mine)
        return pltpu.make_async_remote_copy(
            measured_ref, seen.at[part], seen_send.at[peer], seen_recv.at[slot],
            device_id=(beam, height, peer), device_id_type=MESH,
        )

    for step in range(1, groups):
        info_copy(step, group).start()
    for step in range(1, groups):
        seen_copy(step, group).start()
    info[pl.ds(group * mine, mine)] = info_ref[...]
    seen[pl.ds(group * mine, mine)] = measured_ref[...]

    fetches = [
        pltpu.make_async_copy(maps_ref.at[:, x], current.at[x], maps_sem.at[x]) for x in range(depth)
    ]
    for fetch in fetches:
        fetch.start()
    tail = tail_rows(rows, elems, False)
    for part, out_ref in zip(split(table_ref[...]), (out_high, out_low)):
        tiled, bodies = tile_blocks(part, rows, elems)
        incident_rows = jnp.concatenate([tiled[elems:]] * ((GROUP + 8) // 8), axis=0)
        out_ref[...] = jnp.concatenate(bodies + [tail * incident_rows], axis=0).astype(BF16)
    _, bodies = tile_blocks(turned_ref[...].astype(BF16), rows, elems)
    back_high[...] = jnp.concatenate(bodies + [tail_rows(rows, elems, True)], axis=0).astype(BF16)
    source_at = lax.broadcasted_iota(jnp.int32, (width, width), 0)
    exit_at = lax.broadcasted_iota(jnp.int32, (width, width), 1)
    half = jnp.where(source_at == exit_at, 0.5, 0.0)
    exit_ref[...] = jnp.where(source_at > exit_at, 1.0, half).astype(BF16)
    enter_ref[...] = jnp.where(source_at < exit_at, 1.0, half).astype(BF16)
    for x in range(depth):
        fetches[x].wait()
        shifted[x] = pltpu.roll(current[x], width - 1, 1)

    for step in range(1, groups):
        copy = info_copy(step, lax.rem(group + step, groups))
        copy.wait_send()
        copy.wait_recv()
    fill = pltpu.make_async_copy(info, scalars, local_sem)
    fill.start()
    fill.wait()

    def slab_copy(iteration, a, step, slot):
        peer = lax.rem(beam + step, beams)
        return pltpu.make_async_remote_copy(
            slabs.at[iteration, beam, a], slabs.at[iteration, slot, a],
            slab_send.at[iteration, peer, a], slab_recv.at[iteration, slot, a],
            device_id=(peer, height, group), device_id_type=MESH,
        )

    def norm_copy(iteration, step, slot):
        peer = lax.rem(place + step, plane)
        return pltpu.make_async_remote_copy(
            squares.at[iteration, place], squares.at[iteration, slot],
            norm_send.at[iteration, peer], norm_recv.at[iteration, slot],
            device_id=plane_id(peer), device_id_type=MESH,
        )

    def forward(iteration, a):
        cols = info[a]
        start = jnp.broadcast_to(cols[:, 0:1], (depth, width))
        fraction = cols[:, 1:2]
        path = cols[0:1, 2:3]
        position = lax.broadcasted_iota(jnp.int32, (depth, width), 1).astype(F32)
        below = start < 0
        inside = (below & (position <= (width - 1) + start)) | (~below & (position >= start))
        edge = below & (position == width - 1) & (start >= -width)
        inner = inside & (position <= width - 2)
        coef0[a] = jnp.where(inside, 1.0 - fraction, 0.0)
        coef1[a] = jnp.where(inner | edge, fraction, 0.0)
        for x in range(depth):
            blend = coef0[a, x : x + 1] * current[x] + coef1[a, x : x + 1] * shifted[x]
            shift = scalars[a, x, 3].astype(jnp.int32)
            sampled[a, x * elems : (x + 1) * elems] = pltpu.roll(blend, shift, 1)
        return path

    def forward_pair(iteration, pair):
        paths = [forward(iteration, a) for a in pair]
        carries = [jnp.zeros((1, width), F32) for _ in pair]
        totals = [jnp.zeros((elems, width), F32) for _ in pair]
        for g in range(xgroups):
            depths = []
            for n, a in enumerate(pair):
                mu = mix(out_high, out_low, sampled[a, g * rows : (g + 1) * rows])
                depth_in = paths[n] * mu[rows : rows + GROUP] + carries[n]
                carries[n] = carries[n] + paths[n] * mu[rows + GROUP : rows + GROUP + 1]
                depths.append((depth_in, spread(mu[:rows], exit_ref[...])))
            for n, a in enumerate(pair):
                depth_in, tau = depths[n]
                for xi in range(GROUP):
                    part = slice((g * GROUP + xi) * elems, (g * GROUP + xi + 1) * elems)
                    fade = jnp.exp(-(tau[xi * elems : (xi + 1) * elems] + depth_in[xi : xi + 1]))
                    fading[a, part] = fade
                    totals[n] = totals[n] + fade * sampled[a, part]
        for n, a in enumerate(pair):
            slabs[iteration, beam, a, 0:elems] = (paths[n] * DETECT_SCALE) * totals[n]
            slabs[iteration, beam, a, elems : elems + 8] = jnp.broadcast_to(carries[n], (8, width))
            for step in range(1, beams):
                slab_copy(iteration, a, step, beam).start()

    def backward(iteration, a):
        for step in range(1, beams):
            copy = slab_copy(iteration, a, step, lax.rem(beam + step, beams))
            copy.wait_send()
            copy.wait_recv()
        cols = info[a]
        path = cols[0:1, 2:3]
        before = jnp.zeros((1, width), F32)
        scale = jnp.zeros((1, width), F32)
        fluor = jnp.zeros((elems, width), F32)
        after = jnp.zeros((elems, width), F32)
        for b in range(beams):
            dim = jnp.exp(-before)
            part = dim * slabs[iteration, b, a, 0:elems]
            fluor = fluor + part
            after = after + jnp.where(b > beam, 1.0, 0.0) * part
            scale = scale + jnp.where(b == beam, 1.0, 0.0) * dim
            before = before + slabs[iteration, b, a, elems : elems + 1]
        residual = fluor - seen[a]
        misfit[a] = residual
        carry = jnp.sum(residual * after, axis=0, keepdims=True)
        source = residual * (scale * (path * DETECT_SCALE))
        incident = path * incident_ref[...]
        return source, incident, carry

    def backward_pair(iteration, pair):
        heads = [backward(iteration, a) for a in pair]
        carries = [head[2] for head in heads]
        for g in reversed(range(xgroups)):
            sensed = []
            for n, a in enumerate(pair):
                source = heads[n][0]
                emitted = []
                for xi in range(GROUP):
                    x = g * GROUP + xi
                    part = slice(x * elems, (x + 1) * elems)
                    emitted.append(source * fading[a, part] * sampled[a, part])
                mixed = mix_once(back_high, jnp.concatenate(emitted, axis=0))
                behind = mixed[rows : rows + GROUP] + carries[n]
                carries[n] = carries[n] + mixed[rows + GROUP : rows + GROUP + 1]
                sensed.append((behind, spread_once(mixed[:rows], enter_ref[...])))
            for xi in range(GROUP):
                x = g * GROUP + xi
                sum0, sum1 = acc0[x], acc1[x]
                for n, a in enumerate(pair):
                    source, incident, _ = heads[n]
                    behind, back = sensed[n]
                    grad = (
                        source * fading[a, x * elems : (x + 1) * elems]
                        - incident * behind[xi : xi + 1]
                        - back[xi * elems : (xi + 1) * elems]
                    )
                    grad = pltpu.roll(grad, scalars[a, x, 4].astype(jnp.int32), 1)
                    sum0 = sum0 + coef0[a, x : x + 1] * grad
                    sum1 = sum1 + coef1[a, x : x + 1] * grad
                acc0[x] = sum0
                acc1[x] = sum1

    @pl.loop(0, ITERS)
    def _(iteration):
        @pl.loop(0, total_angles // pairs)
        def _(step):
            forward_pair(iteration, [step * pairs + n for n in range(pairs)])

        @pl.when(iteration == 0)
        def _():
            for step in range(1, groups):
                copy = seen_copy(step, lax.rem(group + step, groups))
                copy.wait_send()
                copy.wait_recv()

        acc0[...] = jnp.zeros_like(acc0)
        acc1[...] = jnp.zeros_like(acc1)

        @pl.loop(0, total_angles // pairs)
        def _(step):
            backward_pair(iteration, [step * pairs + n for n in range(pairs)])

        square = jnp.zeros((8, width), F32)
        for x in range(depth):
            grad = acc0[x] + pltpu.roll(acc1[x], 1, 1)
            acc0[x] = grad
            grad = grad * grad
            for row in range(0, elems, 8):
                square = square + grad[row : row + 8]
        folded = square[:, 0:128]
        for lane in range(128, width, 128):
            folded = folded + square[:, lane : lane + 128]
        squares[iteration, place] = folded

        @pl.loop(1, plane)
        def _(step):
            norm_copy(iteration, step, place).start()

        @pl.loop(1, plane)
        def _(step):
            copy = norm_copy(iteration, step, lax.rem(place + step, plane))
            copy.wait_send()
            copy.wait_recv()

        whole = jnp.sum(squares[iteration], axis=0)
        whole = jnp.sum(jnp.sum(whole, axis=0, keepdims=True), axis=1, keepdims=True)
        rate = STEP_SIZE / jnp.sqrt(whole / cells + EPSILON)
        for x in range(depth):
            plane_x = current[x] - rate * acc0[x]
            current[x] = plane_x
            shifted[x] = pltpu.roll(plane_x, width - 1, 1)

    residual_ref[...] = misfit[pl.ds(group * mine, mine)]


def shards(element_maps, angles, absorb_incident, absorb_table, line_index, measured):
    elems, height_rows, depth, width = element_maps.shape
    beams = lax.axis_size("beam")
    heights = lax.axis_size("height")
    groups = lax.axis_size("angles")
    mine = angles.shape[0]
    total_angles = groups * mine
    line_total = depth * beams
    rows = GROUP * elems

    pick_line = (line_index[:, None] == jnp.arange(absorb_table.shape[0])[None, :]).astype(F32)
    absorb_out = jnp.dot(pick_line, absorb_table, precision=HIGHEST)
    table = jnp.concatenate(
        [absorb_out, jnp.broadcast_to(absorb_incident[None, :], (8, elems))], axis=0
    )
    x_pos = (lax.axis_index("beam") * depth + jnp.arange(depth)).astype(F32) - (line_total - 1) / 2
    angle_rad = ((angles.astype(F32) + 0.5) / WINDOW - 0.5) * (math.pi / 2)
    slopes = jnp.tan(angle_rad)
    path_len = 1.0 / jnp.cos(angle_rad)
    shift = x_pos[None, :] * slopes[:, None]
    start = jnp.floor(shift)
    fraction = shift - start
    lanes = jnp.arange(128)[None, None, :]
    info = jnp.zeros((mine, depth, 128), F32)
    columns = (
        start,
        fraction,
        jnp.broadcast_to(path_len[:, None], start.shape),
        jnp.mod(-start, float(width)),
        jnp.mod(start, float(width)),
    )
    for lane, column in enumerate(columns):
        info = jnp.where(lanes == lane, column[:, :, None], info)

    maps = element_maps[:, 0]
    vmem = pl.BlockSpec(memory_space=pltpu.VMEM)
    plane = beams * heights
    updated, residual = pl.pallas_call(
        functools.partial(kernel, (beams, heights, groups)),
        out_shape=(
            jax.ShapeDtypeStruct((depth, elems, width), F32),
            jax.ShapeDtypeStruct((mine, elems, width), F32),
        ),
        in_specs=[pl.BlockSpec(memory_space=pl.ANY)] + [vmem] * 5,
        out_specs=(vmem, vmem),
        scratch_shapes=[
            pltpu.VMEM((depth, elems, width), F32),
            pltpu.VMEM((total_angles, depth, 128), F32),
            pltpu.VMEM((total_angles, elems, width), F32),
            pltpu.SMEM((total_angles, depth, 128), F32),
            pltpu.VMEM((total_angles, depth, width), F32),
            pltpu.VMEM((total_angles, depth, width), F32),
            pltpu.VMEM((total_angles, depth * elems, width), F32),
            pltpu.VMEM((total_angles, depth * elems, width), F32),
            pltpu.VMEM((ITERS, beams, total_angles, elems + 8, width), F32),
            pltpu.VMEM((total_angles, elems, width), F32),
            pltpu.VMEM((depth, elems, width), F32),
            pltpu.VMEM((depth, elems, width), F32),
            pltpu.VMEM((ITERS, plane, 8, 128), F32),
            pltpu.VMEM((rows + GROUP + 8, rows), BF16),
            pltpu.VMEM((rows + GROUP + 8, rows), BF16),
            pltpu.VMEM((rows + GROUP + 8, rows), BF16),
            pltpu.VMEM((width, width), BF16),
            pltpu.VMEM((width, width), BF16),
            pltpu.SemaphoreType.DMA,
            pltpu.SemaphoreType.DMA((depth,)),
            pltpu.SemaphoreType.DMA((groups,)),
            pltpu.SemaphoreType.DMA((groups,)),
            pltpu.SemaphoreType.DMA((groups,)),
            pltpu.SemaphoreType.DMA((groups,)),
            pltpu.SemaphoreType.DMA((ITERS, beams, total_angles)),
            pltpu.SemaphoreType.DMA((ITERS, beams, total_angles)),
            pltpu.SemaphoreType.DMA((ITERS, plane)),
            pltpu.SemaphoreType.DMA((ITERS, plane)),
        ],
        compiler_params=pltpu.CompilerParams(
            collective_id=0, has_side_effects=True, vmem_limit_bytes=40 * 1024 * 1024
        ),
    )(
        maps, info, measured[:, :, 0], jnp.broadcast_to(absorb_incident[:, None], (elems, width)),
        table, absorb_out.T,
    )
    return (jnp.transpose(updated, (1, 0, 2))[:, None], residual[:, :, None])


def solution(mesh):
    in_specs = (
        P(None, "height", "beam", None),
        P("angles"),
        P(),
        P(),
        P(),
        P("angles", None, "height", None),
    )
    out_specs = (P(None, "height", "beam", None), P("angles", None, "height", None))
    return jax.shard_map(shards, mesh=mesh, in_specs=in_specs, out_specs=out_specs, check_vma=False)
```

```python
import functools
import math

import jax
import jax.numpy as jnp
from jax import lax
from jax.experimental import pallas as pl
from jax.experimental.pallas import tpu as pltpu
from jax.sharding import PartitionSpec as P

WINDOW = 96
ITERS = 2
EPSILON = 1e-06
STEP_SIZE = 0.05
DETECT_SCALE = 1.0 / 32.0
HIGHEST = lax.Precision.HIGHEST
MESH = pl.DeviceIdType.MESH
F32 = jnp.float32
BF16 = jnp.bfloat16
GROUP = 8


def split(value):
    high = value.astype(BF16)
    return high, (value - high.astype(F32)).astype(BF16)


def dot(left, right):
    return jnp.dot(left, right, preferred_element_type=F32)


def mix(high_ref, low_ref, value):
    high, low = split(value)
    return dot(high_ref[...], high) + (dot(low_ref[...], high) + dot(high_ref[...], low))


def mix_once(table_ref, value):
    return dot(table_ref[...], value.astype(BF16))


def spread_once(value, sums):
    return dot(value.astype(BF16), sums)


def tile_blocks(table, rows, elems):
    lane = lax.broadcasted_iota(jnp.int32, (elems, rows), 1)
    row = lax.broadcasted_iota(jnp.int32, (elems, rows), 0)
    repeat = jnp.zeros((elems, rows), F32)
    for block in range(GROUP):
        repeat = jnp.where(lane == row + block * elems, 1.0, repeat)
    tiled = dot(table, repeat.astype(BF16))
    lane = lax.broadcasted_iota(jnp.int32, tiled.shape, 1)
    bodies = [
        jnp.where((lane >= block * elems) & (lane < (block + 1) * elems), tiled, 0.0)[:elems]
        for block in range(GROUP)
    ]
    return tiled, bodies


def tail_rows(rows, elems, backward):
    lane = lax.broadcasted_iota(jnp.int32, (GROUP + 8, rows), 1)
    row = lax.broadcasted_iota(jnp.int32, (GROUP + 8, rows), 0)
    block = jnp.zeros((GROUP + 8, rows), jnp.int32)
    for step in range(1, GROUP):
        block = block + jnp.where(lane >= step * elems, 1, 0)
    ahead = block > row if backward else block < row
    weight = jnp.where(ahead, 1.0, jnp.where(block == row, 0.5, 0.0))
    return jnp.where(row < GROUP, weight, 1.0)


def spread(value, sums):
    high, low = split(value)
    return dot(high, sums) + dot(low, sums)


def kernel(
    sizes,
    maps_ref, info_ref, measured_ref, incident_ref, table_ref, turned_ref,
    current, residual_ref,
    shifted, info, seen, scalars, coef0, coef1, sampled, fading, slabs, misfit,
    acc0, acc1, squares, out_high, out_low, back_high, exit_ref, enter_ref,
    local_sem, maps_sem, info_send, info_recv, seen_send, seen_recv,
    slab_send, slab_recv, norm_send, norm_recv,
):
    beams, heights, groups = sizes
    elems, depth, width = maps_ref.shape
    mine = info_ref.shape[0]
    total_angles = groups * mine
    xgroups = depth // GROUP
    pairs = math.gcd(mine, 2)
    turns = mine // pairs
    rows = GROUP * elems
    beam = lax.axis_index("beam")
    height = lax.axis_index("height")
    group = lax.axis_index("angles")
    plane = beams * heights
    place = beam * heights + height
    cells = float(elems * depth * width * plane)

    def plane_id(index):
        return (index // heights, lax.rem(index, heights), group)

    barrier = pltpu.get_barrier_semaphore()
    for step in range(1, groups):
        pl.semaphore_signal(
            barrier, inc=1, device_id=(beam, height, lax.rem(group + step, groups)), device_id_type=MESH
        )

    @pl.loop(1, plane)
    def _(step):
        pl.semaphore_signal(
            barrier, inc=1, device_id=plane_id(lax.rem(place + step, plane)), device_id_type=MESH
        )

    pl.semaphore_wait(barrier, groups - 1 + plane - 1)

    def info_copy(step, slot):
        peer = lax.rem(group + step, groups)
        part = pl.ds(slot * mine, mine)
        return pltpu.make_async_remote_copy(
            info_ref, info.at[part], info_send.at[peer], info_recv.at[slot],
            device_id=(beam, height, peer), device_id_type=MESH,
        )

    def seen_copy(step, slot):
        peer = lax.rem(group + step, groups)
        part = pl.ds(slot * mine, mine)
        return pltpu.make_async_remote_copy(
            measured_ref, seen.at[part], seen_send.at[peer], seen_recv.at[slot],
            device_id=(beam, height, peer), device_id_type=MESH,
        )

    for step in range(1, groups):
        info_copy(step, group).start()
    for step in range(1, groups):
        seen_copy(step, group).start()
    info[pl.ds(group * mine, mine)] = info_ref[...]
    seen[pl.ds(group * mine, mine)] = measured_ref[...]

    fetches = [
        pltpu.make_async_copy(maps_ref.at[:, x], current.at[x], maps_sem.at[x]) for x in range(depth)
    ]
    for fetch in fetches:
        fetch.start()
    tail = tail_rows(rows, elems, False)
    for part, out_ref in zip(split(table_ref[...]), (out_high, out_low)):
        tiled, bodies = tile_blocks(part, rows, elems)
        incident_rows = jnp.concatenate([tiled[elems:]] * ((GROUP + 8) // 8), axis=0)
        out_ref[...] = jnp.concatenate(bodies + [tail * incident_rows], axis=0).astype(BF16)
    _, bodies = tile_blocks(turned_ref[...].astype(BF16), rows, elems)
    back_high[...] = jnp.concatenate(bodies + [tail_rows(rows, elems, True)], axis=0).astype(BF16)
    source_at = lax.broadcasted_iota(jnp.int32, (width, width), 0)
    exit_at = lax.broadcasted_iota(jnp.int32, (width, width), 1)
    half = jnp.where(source_at == exit_at, 0.5, 0.0)
    exit_ref[...] = jnp.where(source_at > exit_at, 1.0, half).astype(BF16)
    enter_ref[...] = jnp.where(source_at < exit_at, 1.0, half).astype(BF16)
    for x in range(depth):
        fetches[x].wait()
        shifted[x] = pltpu.roll(current[x], width - 1, 1)

    def slab_copy(iteration, a, step, slot):
        peer = lax.rem(beam + step, beams)
        return pltpu.make_async_remote_copy(
            slabs.at[iteration, beam, a], slabs.at[iteration, slot, a],
            slab_send.at[iteration, peer, a], slab_recv.at[iteration, slot, a],
            device_id=(peer, height, group), device_id_type=MESH,
        )

    def norm_copy(iteration, step, slot):
        peer = lax.rem(place + step, plane)
        return pltpu.make_async_remote_copy(
            squares.at[iteration, place], squares.at[iteration, slot],
            norm_send.at[iteration, peer], norm_recv.at[iteration, slot],
            device_id=plane_id(peer), device_id_type=MESH,
        )

    def forward(iteration, a):
        cols = info[a]
        start = jnp.broadcast_to(cols[:, 0:1], (depth, width))
        fraction = cols[:, 1:2]
        path = cols[0:1, 2:3]
        position = lax.broadcasted_iota(jnp.int32, (depth, width), 1).astype(F32)
        below = start < 0
        inside = (below & (position <= (width - 1) + start)) | (~below & (position >= start))
        edge = below & (position == width - 1) & (start >= -width)
        inner = inside & (position <= width - 2)
        coef0[a] = jnp.where(inside, 1.0 - fraction, 0.0)
        coef1[a] = jnp.where(inner | edge, fraction, 0.0)
        for x in range(depth):
            blend = coef0[a, x : x + 1] * current[x] + coef1[a, x : x + 1] * shifted[x]
            shift = scalars[a, x, 3].astype(jnp.int32)
            sampled[a, x * elems : (x + 1) * elems] = pltpu.roll(blend, shift, 1)
        return path

    def forward_pair(iteration, pair):
        paths = [forward(iteration, a) for a in pair]
        carries = [jnp.zeros((1, width), F32) for _ in pair]
        totals = [jnp.zeros((elems, width), F32) for _ in pair]
        for g in range(xgroups):
            depths = []
            for n, a in enumerate(pair):
                mu = mix(out_high, out_low, sampled[a, g * rows : (g + 1) * rows])
                depth_in = paths[n] * mu[rows : rows + GROUP] + carries[n]
                carries[n] = carries[n] + paths[n] * mu[rows + GROUP : rows + GROUP + 1]
                depths.append((depth_in, spread(mu[:rows], exit_ref[...])))
            for n, a in enumerate(pair):
                depth_in, tau = depths[n]
                for xi in range(GROUP):
                    part = slice((g * GROUP + xi) * elems, (g * GROUP + xi + 1) * elems)
                    fade = jnp.exp(-(tau[xi * elems : (xi + 1) * elems] + depth_in[xi : xi + 1]))
                    fading[a, part] = fade
                    totals[n] = totals[n] + fade * sampled[a, part]
        for n, a in enumerate(pair):
            slabs[iteration, beam, a, 0:elems] = (paths[n] * DETECT_SCALE) * totals[n]
            slabs[iteration, beam, a, elems : elems + 8] = jnp.broadcast_to(carries[n], (8, width))
            for step in range(1, beams):
                slab_copy(iteration, a, step, beam).start()

    def backward(iteration, a):
        for step in range(1, beams):
            copy = slab_copy(iteration, a, step, lax.rem(beam + step, beams))
            copy.wait_send()
            copy.wait_recv()
        cols = info[a]
        path = cols[0:1, 2:3]
        before = jnp.zeros((1, width), F32)
        scale = jnp.zeros((1, width), F32)
        fluor = jnp.zeros((elems, width), F32)
        after = jnp.zeros((elems, width), F32)
        for b in range(beams):
            dim = jnp.exp(-before)
            part = dim * slabs[iteration, b, a, 0:elems]
            fluor = fluor + part
            after = after + jnp.where(b > beam, 1.0, 0.0) * part
            scale = scale + jnp.where(b == beam, 1.0, 0.0) * dim
            before = before + slabs[iteration, b, a, elems : elems + 1]
        residual = fluor - seen[a]
        misfit[a] = residual
        carry = jnp.sum(residual * after, axis=0, keepdims=True)
        source = residual * (scale * (path * DETECT_SCALE))
        incident = path * incident_ref[...]
        return source, incident, carry

    def backward_pair(iteration, pair):
        heads = [backward(iteration, a) for a in pair]
        carries = [head[2] for head in heads]
        for g in reversed(range(xgroups)):
            sensed = []
            for n, a in enumerate(pair):
                source = heads[n][0]
                emitted = []
                for xi in range(GROUP):
                    x = g * GROUP + xi
                    part = slice(x * elems, (x + 1) * elems)
                    emitted.append(source * fading[a, part] * sampled[a, part])
                mixed = mix_once(back_high, jnp.concatenate(emitted, axis=0))
                behind = mixed[rows : rows + GROUP] + carries[n]
                carries[n] = carries[n] + mixed[rows + GROUP : rows + GROUP + 1]
                sensed.append((behind, spread_once(mixed[:rows], enter_ref[...])))
            for xi in range(GROUP):
                x = g * GROUP + xi
                sum0, sum1 = acc0[x], acc1[x]
                for n, a in enumerate(pair):
                    source, incident, _ = heads[n]
                    behind, back = sensed[n]
                    grad = (
                        source * fading[a, x * elems : (x + 1) * elems]
                        - incident * behind[xi : xi + 1]
                        - back[xi * elems : (xi + 1) * elems]
                    )
                    grad = pltpu.roll(grad, scalars[a, x, 4].astype(jnp.int32), 1)
                    sum0 = sum0 + coef0[a, x : x + 1] * grad
                    sum1 = sum1 + coef1[a, x : x + 1] * grad
                acc0[x] = sum0
                acc1[x] = sum1

    @pl.loop(0, ITERS)
    def _(iteration):
        @pl.loop(0, total_angles // pairs)
        def _(step):
            first = lax.rem(group * mine + step * pairs, total_angles)

            @pl.when((iteration == 0) & (lax.rem(step, turns) == 0))
            def _():
                slot = first // mine

                @pl.when(step >= turns)
                def _():
                    copy = info_copy(step // turns, slot)
                    copy.wait_send()
                    copy.wait_recv()

                part = pl.ds(slot * mine, mine)
                fill = pltpu.make_async_copy(info.at[part], scalars.at[part], local_sem)
                fill.start()
                fill.wait()

            forward_pair(iteration, [first + n for n in range(pairs)])

        @pl.when(iteration == 0)
        def _():
            for step in range(1, groups):
                copy = seen_copy(step, lax.rem(group + step, groups))
                copy.wait_send()
                copy.wait_recv()

        acc0[...] = jnp.zeros_like(acc0)
        acc1[...] = jnp.zeros_like(acc1)

        @pl.loop(0, total_angles // pairs)
        def _(step):
            backward_pair(iteration, [step * pairs + n for n in range(pairs)])

        square = jnp.zeros((8, width), F32)
        for x in range(depth):
            grad = acc0[x] + pltpu.roll(acc1[x], 1, 1)
            acc0[x] = grad
            grad = grad * grad
            for row in range(0, elems, 8):
                square = square + grad[row : row + 8]
        folded = square[:, 0:128]
        for lane in range(128, width, 128):
            folded = folded + square[:, lane : lane + 128]
        squares[iteration, place] = folded

        @pl.loop(1, plane)
        def _(step):
            norm_copy(iteration, step, place).start()

        @pl.loop(1, plane)
        def _(step):
            copy = norm_copy(iteration, step, lax.rem(place + step, plane))
            copy.wait_send()
            copy.wait_recv()

        whole = jnp.sum(squares[iteration], axis=0)
        whole = jnp.sum(jnp.sum(whole, axis=0, keepdims=True), axis=1, keepdims=True)
        rate = STEP_SIZE / jnp.sqrt(whole / cells + EPSILON)
        for x in range(depth):
            plane_x = current[x] - rate * acc0[x]
            current[x] = plane_x
            shifted[x] = pltpu.roll(plane_x, width - 1, 1)

    residual_ref[...] = misfit[pl.ds(group * mine, mine)]


def shards(element_maps, angles, absorb_incident, absorb_table, line_index, measured):
    elems, height_rows, depth, width = element_maps.shape
    beams = lax.axis_size("beam")
    heights = lax.axis_size("height")
    groups = lax.axis_size("angles")
    mine = angles.shape[0]
    total_angles = groups * mine
    line_total = depth * beams
    rows = GROUP * elems

    pick_line = (line_index[:, None] == jnp.arange(absorb_table.shape[0])[None, :]).astype(F32)
    absorb_out = jnp.dot(pick_line, absorb_table, precision=HIGHEST)
    table = jnp.concatenate(
        [absorb_out, jnp.broadcast_to(absorb_incident[None, :], (8, elems))], axis=0
    )
    x_pos = (lax.axis_index("beam") * depth + jnp.arange(depth)).astype(F32) - (line_total - 1) / 2
    angle_rad = ((angles.astype(F32) + 0.5) / WINDOW - 0.5) * (math.pi / 2)
    slopes = jnp.tan(angle_rad)
    path_len = 1.0 / jnp.cos(angle_rad)
    shift = x_pos[None, :] * slopes[:, None]
    start = jnp.floor(shift)
    fraction = shift - start
    lanes = jnp.arange(128)[None, None, :]
    info = jnp.zeros((mine, depth, 128), F32)
    columns = (
        start,
        fraction,
        jnp.broadcast_to(path_len[:, None], start.shape),
        jnp.mod(-start, float(width)),
        jnp.mod(start, float(width)),
    )
    for lane, column in enumerate(columns):
        info = jnp.where(lanes == lane, column[:, :, None], info)

    maps = element_maps[:, 0]
    vmem = pl.BlockSpec(memory_space=pltpu.VMEM)
    plane = beams * heights
    updated, residual = pl.pallas_call(
        functools.partial(kernel, (beams, heights, groups)),
        out_shape=(
            jax.ShapeDtypeStruct((depth, elems, width), F32),
            jax.ShapeDtypeStruct((mine, elems, width), F32),
        ),
        in_specs=[pl.BlockSpec(memory_space=pl.ANY)] + [vmem] * 5,
        out_specs=(vmem, vmem),
        scratch_shapes=[
            pltpu.VMEM((depth, elems, width), F32),
            pltpu.VMEM((total_angles, depth, 128), F32),
            pltpu.VMEM((total_angles, elems, width), F32),
            pltpu.SMEM((total_angles, depth, 128), F32),
            pltpu.VMEM((total_angles, depth, width), F32),
            pltpu.VMEM((total_angles, depth, width), F32),
            pltpu.VMEM((total_angles, depth * elems, width), F32),
            pltpu.VMEM((total_angles, depth * elems, width), F32),
            pltpu.VMEM((ITERS, beams, total_angles, elems + 8, width), F32),
            pltpu.VMEM((total_angles, elems, width), F32),
            pltpu.VMEM((depth, elems, width), F32),
            pltpu.VMEM((depth, elems, width), F32),
            pltpu.VMEM((ITERS, plane, 8, 128), F32),
            pltpu.VMEM((rows + GROUP + 8, rows), BF16),
            pltpu.VMEM((rows + GROUP + 8, rows), BF16),
            pltpu.VMEM((rows + GROUP + 8, rows), BF16),
            pltpu.VMEM((width, width), BF16),
            pltpu.VMEM((width, width), BF16),
            pltpu.SemaphoreType.DMA,
            pltpu.SemaphoreType.DMA((depth,)),
            pltpu.SemaphoreType.DMA((groups,)),
            pltpu.SemaphoreType.DMA((groups,)),
            pltpu.SemaphoreType.DMA((groups,)),
            pltpu.SemaphoreType.DMA((groups,)),
            pltpu.SemaphoreType.DMA((ITERS, beams, total_angles)),
            pltpu.SemaphoreType.DMA((ITERS, beams, total_angles)),
            pltpu.SemaphoreType.DMA((ITERS, plane)),
            pltpu.SemaphoreType.DMA((ITERS, plane)),
        ],
        compiler_params=pltpu.CompilerParams(
            collective_id=0, has_side_effects=True, vmem_limit_bytes=40 * 1024 * 1024
        ),
    )(
        maps, info, measured[:, :, 0], jnp.broadcast_to(absorb_incident[:, None], (elems, width)),
        table, absorb_out.T,
    )
    return (jnp.transpose(updated, (1, 0, 2))[:, None], residual[:, :, None])


def solution(mesh):
    in_specs = (
        P(None, "height", "beam", None),
        P("angles"),
        P(),
        P(),
        P(),
        P("angles", None, "height", None),
    )
    out_specs = (P(None, "height", "beam", None), P("angles", None, "height", None))
    return jax.shard_map(shards, mesh=mesh, in_specs=in_specs, out_specs=out_specs, check_vma=False)
```

```python
import functools
import math

import jax
import jax.numpy as jnp
from jax import lax
from jax.experimental import pallas as pl
from jax.experimental.pallas import tpu as pltpu
from jax.sharding import PartitionSpec as P

WINDOW = 96
ITERS = 2
EPSILON = 1e-06
STEP_SIZE = 0.05
DETECT_SCALE = 1.0 / 32.0
HIGHEST = lax.Precision.HIGHEST
MESH = pl.DeviceIdType.MESH
F32 = jnp.float32
BF16 = jnp.bfloat16
GROUP = 8


def split(value):
    high = value.astype(BF16)
    return high, (value - high.astype(F32)).astype(BF16)


def dot(left, right):
    return jnp.dot(left, right, preferred_element_type=F32)


def mix(high_ref, low_ref, value):
    high, low = split(value)
    return dot(high_ref[...], high) + (dot(low_ref[...], high) + dot(high_ref[...], low))


def mix_once(table_ref, value):
    return dot(table_ref[...], value.astype(BF16))


def spread_once(value, sums):
    return dot(value.astype(BF16), sums)


def tile_blocks(table, rows, elems):
    lane = lax.broadcasted_iota(jnp.int32, (elems, rows), 1)
    row = lax.broadcasted_iota(jnp.int32, (elems, rows), 0)
    repeat = jnp.zeros((elems, rows), F32)
    for block in range(GROUP):
        repeat = jnp.where(lane == row + block * elems, 1.0, repeat)
    tiled = dot(table, repeat.astype(BF16))
    lane = lax.broadcasted_iota(jnp.int32, tiled.shape, 1)
    bodies = [
        jnp.where((lane >= block * elems) & (lane < (block + 1) * elems), tiled, 0.0)[:elems]
        for block in range(GROUP)
    ]
    return tiled, bodies


def tail_rows(rows, elems, backward):
    lane = lax.broadcasted_iota(jnp.int32, (GROUP + 8, rows), 1)
    row = lax.broadcasted_iota(jnp.int32, (GROUP + 8, rows), 0)
    block = jnp.zeros((GROUP + 8, rows), jnp.int32)
    for step in range(1, GROUP):
        block = block + jnp.where(lane >= step * elems, 1, 0)
    ahead = block > row if backward else block < row
    weight = jnp.where(ahead, 1.0, jnp.where(block == row, 0.5, 0.0))
    return jnp.where(row < GROUP, weight, 1.0)


def spread(value, sums):
    high, low = split(value)
    return dot(high, sums) + dot(low, sums)


def kernel(
    sizes,
    maps_ref, info_ref, measured_ref, incident_ref, table_ref, turned_ref,
    current, residual_ref,
    shifted, info, seen, scalars, coef0, coef1, sampled, fading, slabs, misfit,
    acc0, acc1, squares, out_high, out_low, back_high, exit_ref, enter_ref,
    local_sem, maps_sem, info_send, info_recv, seen_send, seen_recv,
    slab_send, slab_recv, norm_send, norm_recv,
):
    beams, heights, groups = sizes
    elems, depth, width = maps_ref.shape
    mine = info_ref.shape[0]
    total_angles = groups * mine
    xgroups = depth // GROUP
    pairs = math.gcd(total_angles, 2)
    rows = GROUP * elems
    beam = lax.axis_index("beam")
    height = lax.axis_index("height")
    group = lax.axis_index("angles")
    plane = beams * heights
    place = beam * heights + height
    cells = float(elems * depth * width * plane)

    def plane_id(index):
        return (index // heights, lax.rem(index, heights), group)

    barrier = pltpu.get_barrier_semaphore()
    for step in range(1, groups):
        pl.semaphore_signal(
            barrier, inc=1, device_id=(beam, height, lax.rem(group + step, groups)), device_id_type=MESH
        )

    @pl.loop(1, plane)
    def _(step):
        pl.semaphore_signal(
            barrier, inc=1, device_id=plane_id(lax.rem(place + step, plane)), device_id_type=MESH
        )


    fetches = [
        pltpu.make_async_copy(maps_ref.at[:, x], current.at[x], maps_sem.at[x]) for x in range(depth)
    ]
    for fetch in fetches:
        fetch.start()
    tail = tail_rows(rows, elems, False)
    for part, out_ref in zip(split(table_ref[...]), (out_high, out_low)):
        tiled, bodies = tile_blocks(part, rows, elems)
        incident_rows = jnp.concatenate([tiled[elems:]] * ((GROUP + 8) // 8), axis=0)
        out_ref[...] = jnp.concatenate(bodies + [tail * incident_rows], axis=0).astype(BF16)
    pl.semaphore_wait(barrier, groups - 1 + plane - 1)

    def info_copy(step, slot):
        peer = lax.rem(group + step, groups)
        part = pl.ds(slot * mine, mine)
        return pltpu.make_async_remote_copy(
            info_ref, info.at[part], info_send.at[peer], info_recv.at[slot],
            device_id=(beam, height, peer), device_id_type=MESH,
        )

    def seen_copy(step, slot):
        peer = lax.rem(group + step, groups)
        part = pl.ds(slot * mine, mine)
        return pltpu.make_async_remote_copy(
            measured_ref, seen.at[part], seen_send.at[peer], seen_recv.at[slot],
            device_id=(beam, height, peer), device_id_type=MESH,
        )

    for step in range(1, groups):
        info_copy(step, group).start()
    for step in range(1, groups):
        seen_copy(step, group).start()
    info[pl.ds(group * mine, mine)] = info_ref[...]
    seen[pl.ds(group * mine, mine)] = measured_ref[...]

    _, bodies = tile_blocks(turned_ref[...].astype(BF16), rows, elems)
    back_high[...] = jnp.concatenate(bodies + [tail_rows(rows, elems, True)], axis=0).astype(BF16)
    source_at = lax.broadcasted_iota(jnp.int32, (width, width), 0)
    exit_at = lax.broadcasted_iota(jnp.int32, (width, width), 1)
    half = jnp.where(source_at == exit_at, 0.5, 0.0)
    exit_ref[...] = jnp.where(source_at > exit_at, 1.0, half).astype(BF16)
    enter_ref[...] = jnp.where(source_at < exit_at, 1.0, half).astype(BF16)
    for x in range(depth):
        fetches[x].wait()
        shifted[x] = pltpu.roll(current[x], width - 1, 1)

    for step in range(1, groups):
        copy = info_copy(step, lax.rem(group + step, groups))
        copy.wait_send()
        copy.wait_recv()
    fill = pltpu.make_async_copy(info, scalars, local_sem)
    fill.start()
    fill.wait()

    def slab_copy(iteration, a, step, slot):
        peer = lax.rem(beam + step, beams)
        return pltpu.make_async_remote_copy(
            slabs.at[iteration, beam, a], slabs.at[iteration, slot, a],
            slab_send.at[iteration, peer, a], slab_recv.at[iteration, slot, a],
            device_id=(peer, height, group), device_id_type=MESH,
        )

    def norm_copy(iteration, step, slot):
        peer = lax.rem(place + step, plane)
        return pltpu.make_async_remote_copy(
            squares.at[iteration, place], squares.at[iteration, slot],
            norm_send.at[iteration, peer], norm_recv.at[iteration, slot],
            device_id=plane_id(peer), device_id_type=MESH,
        )

    def forward(iteration, a):
        cols = info[a]
        start = jnp.broadcast_to(cols[:, 0:1], (depth, width))
        fraction = cols[:, 1:2]
        path = cols[0:1, 2:3]
        position = lax.broadcasted_iota(jnp.int32, (depth, width), 1).astype(F32)
        below = start < 0
        inside = (below & (position <= (width - 1) + start)) | (~below & (position >= start))
        edge = below & (position == width - 1) & (start >= -width)
        inner = inside & (position <= width - 2)
        coef0[a] = jnp.where(inside, 1.0 - fraction, 0.0)
        coef1[a] = jnp.where(inner | edge, fraction, 0.0)
        for x in range(depth):
            blend = coef0[a, x : x + 1] * current[x] + coef1[a, x : x + 1] * shifted[x]
            shift = scalars[a, x, 3].astype(jnp.int32)
            sampled[a, x * elems : (x + 1) * elems] = pltpu.roll(blend, shift, 1)
        return path

    def forward_pair(iteration, pair):
        paths = [forward(iteration, a) for a in pair]
        carries = [jnp.zeros((1, width), F32) for _ in pair]
        totals = [jnp.zeros((elems, width), F32) for _ in pair]
        for g in range(xgroups):
            depths = []
            for n, a in enumerate(pair):
                mu = mix(out_high, out_low, sampled[a, g * rows : (g + 1) * rows])
                depth_in = paths[n] * mu[rows : rows + GROUP] + carries[n]
                carries[n] = carries[n] + paths[n] * mu[rows + GROUP : rows + GROUP + 1]
                depths.append((depth_in, spread(mu[:rows], exit_ref[...])))
            for n, a in enumerate(pair):
                depth_in, tau = depths[n]
                for xi in range(GROUP):
                    part = slice((g * GROUP + xi) * elems, (g * GROUP + xi + 1) * elems)
                    fade = jnp.exp(-(tau[xi * elems : (xi + 1) * elems] + depth_in[xi : xi + 1]))
                    fading[a, part] = fade
                    totals[n] = totals[n] + fade * sampled[a, part]
        for n, a in enumerate(pair):
            slabs[iteration, beam, a, 0:elems] = (paths[n] * DETECT_SCALE) * totals[n]
            slabs[iteration, beam, a, elems : elems + 8] = jnp.broadcast_to(carries[n], (8, width))
            for step in range(1, beams):
                slab_copy(iteration, a, step, beam).start()

    def backward(iteration, a):
        for step in range(1, beams):
            copy = slab_copy(iteration, a, step, lax.rem(beam + step, beams))
            copy.wait_send()
            copy.wait_recv()
        cols = info[a]
        path = cols[0:1, 2:3]
        before = jnp.zeros((1, width), F32)
        scale = jnp.zeros((1, width), F32)
        fluor = jnp.zeros((elems, width), F32)
        after = jnp.zeros((elems, width), F32)
        for b in range(beams):
            dim = jnp.exp(-before)
            part = dim * slabs[iteration, b, a, 0:elems]
            fluor = fluor + part
            after = after + jnp.where(b > beam, 1.0, 0.0) * part
            scale = scale + jnp.where(b == beam, 1.0, 0.0) * dim
            before = before + slabs[iteration, b, a, elems : elems + 1]
        residual = fluor - seen[a]
        misfit[a] = residual
        carry = jnp.sum(residual * after, axis=0, keepdims=True)
        source = residual * (scale * (path * DETECT_SCALE))
        incident = path * incident_ref[...]
        return source, incident, carry

    def backward_pair(iteration, pair):
        heads = [backward(iteration, a) for a in pair]
        carries = [head[2] for head in heads]
        for g in reversed(range(xgroups)):
            sensed = []
            for n, a in enumerate(pair):
                source = heads[n][0]
                emitted = []
                for xi in range(GROUP):
                    x = g * GROUP + xi
                    part = slice(x * elems, (x + 1) * elems)
                    emitted.append(source * fading[a, part] * sampled[a, part])
                mixed = mix_once(back_high, jnp.concatenate(emitted, axis=0))
                behind = mixed[rows : rows + GROUP] + carries[n]
                carries[n] = carries[n] + mixed[rows + GROUP : rows + GROUP + 1]
                sensed.append((behind, spread_once(mixed[:rows], enter_ref[...])))
            for xi in range(GROUP):
                x = g * GROUP + xi
                sum0, sum1 = acc0[x], acc1[x]
                for n, a in enumerate(pair):
                    source, incident, _ = heads[n]
                    behind, back = sensed[n]
                    grad = (
                        source * fading[a, x * elems : (x + 1) * elems]
                        - incident * behind[xi : xi + 1]
                        - back[xi * elems : (xi + 1) * elems]
                    )
                    grad = pltpu.roll(grad, scalars[a, x, 4].astype(jnp.int32), 1)
                    sum0 = sum0 + coef0[a, x : x + 1] * grad
                    sum1 = sum1 + coef1[a, x : x + 1] * grad
                acc0[x] = sum0
                acc1[x] = sum1

    @pl.loop(0, ITERS)
    def _(iteration):
        @pl.loop(0, total_angles // pairs)
        def _(step):
            forward_pair(iteration, [step * pairs + n for n in range(pairs)])

        @pl.when(iteration == 0)
        def _():
            for step in range(1, groups):
                copy = seen_copy(step, lax.rem(group + step, groups))
                copy.wait_send()
                copy.wait_recv()

        acc0[...] = jnp.zeros_like(acc0)
        acc1[...] = jnp.zeros_like(acc1)

        @pl.loop(0, total_angles // pairs)
        def _(step):
            backward_pair(iteration, [step * pairs + n for n in range(pairs)])

        square = jnp.zeros((8, width), F32)
        for x in range(depth):
            grad = acc0[x] + pltpu.roll(acc1[x], 1, 1)
            acc0[x] = grad
            grad = grad * grad
            for row in range(0, elems, 8):
                square = square + grad[row : row + 8]
        folded = square[:, 0:128]
        for lane in range(128, width, 128):
            folded = folded + square[:, lane : lane + 128]
        squares[iteration, place] = folded

        @pl.loop(1, plane)
        def _(step):
            norm_copy(iteration, step, place).start()

        @pl.loop(1, plane)
        def _(step):
            copy = norm_copy(iteration, step, lax.rem(place + step, plane))
            copy.wait_send()
            copy.wait_recv()

        whole = jnp.sum(squares[iteration], axis=0)
        whole = jnp.sum(jnp.sum(whole, axis=0, keepdims=True), axis=1, keepdims=True)
        rate = STEP_SIZE / jnp.sqrt(whole / cells + EPSILON)
        for x in range(depth):
            plane_x = current[x] - rate * acc0[x]
            current[x] = plane_x
            shifted[x] = pltpu.roll(plane_x, width - 1, 1)

    residual_ref[...] = misfit[pl.ds(group * mine, mine)]


def shards(element_maps, angles, absorb_incident, absorb_table, line_index, measured):
    elems, height_rows, depth, width = element_maps.shape
    beams = lax.axis_size("beam")
    heights = lax.axis_size("height")
    groups = lax.axis_size("angles")
    mine = angles.shape[0]
    total_angles = groups * mine
    line_total = depth * beams
    rows = GROUP * elems

    pick_line = (line_index[:, None] == jnp.arange(absorb_table.shape[0])[None, :]).astype(F32)
    absorb_out = jnp.dot(pick_line, absorb_table, precision=HIGHEST)
    table = jnp.concatenate(
        [absorb_out, jnp.broadcast_to(absorb_incident[None, :], (8, elems))], axis=0
    )
    x_pos = (lax.axis_index("beam") * depth + jnp.arange(depth)).astype(F32) - (line_total - 1) / 2
    angle_rad = ((angles.astype(F32) + 0.5) / WINDOW - 0.5) * (math.pi / 2)
    slopes = jnp.tan(angle_rad)
    path_len = 1.0 / jnp.cos(angle_rad)
    shift = x_pos[None, :] * slopes[:, None]
    start = jnp.floor(shift)
    fraction = shift - start
    lanes = jnp.arange(128)[None, None, :]
    info = jnp.zeros((mine, depth, 128), F32)
    columns = (
        start,
        fraction,
        jnp.broadcast_to(path_len[:, None], start.shape),
        jnp.mod(-start, float(width)),
        jnp.mod(start, float(width)),
    )
    for lane, column in enumerate(columns):
        info = jnp.where(lanes == lane, column[:, :, None], info)

    maps = element_maps[:, 0]
    vmem = pl.BlockSpec(memory_space=pltpu.VMEM)
    plane = beams * heights
    updated, residual = pl.pallas_call(
        functools.partial(kernel, (beams, heights, groups)),
        out_shape=(
            jax.ShapeDtypeStruct((depth, elems, width), F32),
            jax.ShapeDtypeStruct((mine, elems, width), F32),
        ),
        in_specs=[pl.BlockSpec(memory_space=pl.ANY)] + [vmem] * 5,
        out_specs=(vmem, vmem),
        scratch_shapes=[
            pltpu.VMEM((depth, elems, width), F32),
            pltpu.VMEM((total_angles, depth, 128), F32),
            pltpu.VMEM((total_angles, elems, width), F32),
            pltpu.SMEM((total_angles, depth, 128), F32),
            pltpu.VMEM((total_angles, depth, width), F32),
            pltpu.VMEM((total_angles, depth, width), F32),
            pltpu.VMEM((total_angles, depth * elems, width), F32),
            pltpu.VMEM((total_angles, depth * elems, width), F32),
            pltpu.VMEM((ITERS, beams, total_angles, elems + 8, width), F32),
            pltpu.VMEM((total_angles, elems, width), F32),
            pltpu.VMEM((depth, elems, width), F32),
            pltpu.VMEM((depth, elems, width), F32),
            pltpu.VMEM((ITERS, plane, 8, 128), F32),
            pltpu.VMEM((rows + GROUP + 8, rows), BF16),
            pltpu.VMEM((rows + GROUP + 8, rows), BF16),
            pltpu.VMEM((rows + GROUP + 8, rows), BF16),
            pltpu.VMEM((width, width), BF16),
            pltpu.VMEM((width, width), BF16),
            pltpu.SemaphoreType.DMA,
            pltpu.SemaphoreType.DMA((depth,)),
            pltpu.SemaphoreType.DMA((groups,)),
            pltpu.SemaphoreType.DMA((groups,)),
            pltpu.SemaphoreType.DMA((groups,)),
            pltpu.SemaphoreType.DMA((groups,)),
            pltpu.SemaphoreType.DMA((ITERS, beams, total_angles)),
            pltpu.SemaphoreType.DMA((ITERS, beams, total_angles)),
            pltpu.SemaphoreType.DMA((ITERS, plane)),
            pltpu.SemaphoreType.DMA((ITERS, plane)),
        ],
        compiler_params=pltpu.CompilerParams(
            collective_id=0, has_side_effects=True, vmem_limit_bytes=60 * 1024 * 1024
        ),
    )(
        maps, info, measured[:, :, 0], jnp.broadcast_to(absorb_incident[:, None], (elems, width)),
        table, absorb_out.T,
    )
    return (jnp.transpose(updated, (1, 0, 2))[:, None], residual[:, :, None])


def solution(mesh):
    in_specs = (
        P(None, "height", "beam", None),
        P("angles"),
        P(),
        P(),
        P(),
        P("angles", None, "height", None),
    )
    out_specs = (P(None, "height", "beam", None), P("angles", None, "height", None))
    return jax.shard_map(shards, mesh=mesh, in_specs=in_specs, out_specs=out_specs, check_vma=False)
```
